32 devices in a mesh: context: 16 (over z, y, x), tensor: 2 (over core).
Axes of the slice: x: 2, y: 2, z: 4, core: 2. Of those that a mesh axis runs over, the one named last changes fastest.
Arguments:
- query_proj: bfloat16 [2048, 8192], P('context', 'tensor'), may hold values from -6 to 6
- key_proj: bfloat16 [2048, 8192], P('context', 'tensor'), may hold values from -6 to 6
- value_proj: bfloat16 [2048, 8192], P('context', 'tensor'), may hold values from -6 to 6
- short_filter: float32 [3, 7, 8192], P(None, None, 'tensor'), may hold values from -2 to 2
- residues: float32 [16, 8192], P(None, 'tensor'), may hold values from -1.5 to 1.5
- decay: float32 [16, 8192], P(None, 'tensor'), may hold values from 0.00048828125 to 0.033333335
- skip_gain: float32 [8192], P('tensor'), may hold values from -6 to 6
- residual: bfloat16 [2048, 8192], P('context', 'tensor'), may hold values from -50 to 50
- norm_gain: float32 [8192], P('tensor'), may hold values from 0.5 to 1.5
Outputs:
- mixed: bfloat16 [2048, 8192], P('context', 'tensor')
- normed: bfloat16 [2048, 8192], P('context', 'tensor')
The draws below stay inside these ranges and needn't reach their ends.
All inputs are finite; a program needn't handle non-finite values.
Results may differ from the reference program's by a relative error of at most 0.014.
Values may be sent and summed in bfloat16 or wider, within the bound.
A program may use at most 128 MiB of HBM per device.

```python
import math
import jax
import jax.numpy as jnp
from jax import lax

D = 8192
ORDER = 16
SHORT = 7
SEQ = 2048


def draw_residual(key, part):
    row_key, value_key = jax.random.split(key, 2)
    columns = jnp.arange(D).astype(jnp.float32) / D
    row_levels = jax.random.uniform(row_key, (SEQ, 1), jnp.float32)
    factor = jnp.exp(0.5 * math.log(10.0) * (columns[None, :] + row_levels))
    values = jax.random.truncated_normal(value_key, -5.0, 5.0, (SEQ, D), jnp.float32)
    return (values * factor).astype(jnp.bfloat16)


def levels(own_key, dims, shards, smallest, top_value):
    def one(dim, blocks):
        steps = jax.random.uniform(jax.random.fold_in(jax.random.fold_in(own_key, 6), dim), (blocks,), jnp.float32, smallest / len(shards), top_value / len(shards))
        return jnp.repeat(jnp.exp(steps), dims[dim] // blocks).reshape((-1,) + (1,) * (len(dims) - dim - 1))

    factor_of = one(*shards[0])
    for cut in shards[1:]:
        factor_of = factor_of * one(*cut)
    return factor_of


def bell_draw(rng, dims, deviation, limit, cuts=(), kind=jnp.bfloat16):
    values = deviation * jax.random.normal(rng, dims, jnp.float32)
    if cuts:
        values = values * levels(rng, dims, cuts, -0.22, 0.18)
    return jnp.clip(values, -limit, limit).astype(kind)


def setup_inputs(seed: int = 0) -> dict:
    key_list = jax.random.split(jax.random.key(seed), 10)
    query_proj = bell_draw(key_list[0], (SEQ, D), 1.0, 6.0, ((0, 16), (1, 2)))
    key_proj = bell_draw(key_list[1], (SEQ, D), 1.0, 6.0, ((0, 16), (1, 2)))
    value_proj = bell_draw(key_list[2], (SEQ, D), 1.0, 6.0, ((0, 16), (1, 2)))
    short_filter = bell_draw(key_list[3], (3, SHORT, D), SHORT ** -0.5, 2.0, ((2, 2),), jnp.float32)
    residues = bell_draw(key_list[4], (ORDER, D), 0.25, 1.5, ((1, 2),), jnp.float32)
    decay = jnp.clip(jnp.exp(math.log(0.033333335) - 4.2234217 * jax.random.uniform(key_list[5], (ORDER, D), jnp.float32) ** levels(key_list[5], (ORDER, D), ((1, 2),), -0.2, 0.2)), 0.00048828125, 0.033333335)
    skip_gain = bell_draw(key_list[6], (D,), 1.0, 6.0, ((0, 2),), jnp.float32)
    residual = draw_residual(jax.random.fold_in(key_list[9], 71), 0)
    norm_gain = jnp.clip(1.0 + 0.1 * jax.random.normal(key_list[8], (D,), jnp.float32), 0.5, 1.5)
    return {"query_proj": query_proj, "key_proj": key_proj, "value_proj": value_proj, "short_filter": short_filter, "residues": residues, "decay": decay, "skip_gain": skip_gain, "residual": residual, "norm_gain": norm_gain}


def short_conv(signal, taps_table):
    tap_count = taps_table.shape[0]
    padded = jnp.pad(signal, ((tap_count - 1, 0), (0, 0)))
    result = padded[tap_count - 1:] * taps_table[0]
    for offset in range(1, tap_count):
        result = result + padded[tap_count - 1 - offset:tap_count - 1 - offset + SEQ] * taps_table[offset]
    return result

def channel_block(pieces):
    query_b, key_b, value_b, filter_b, residue_b, rate_b, skip_b = pieces
    query_conv = short_conv(query_b.astype(jnp.float32), filter_b[0])
    key_conv = short_conv(key_b.astype(jnp.float32), filter_b[1])
    value_conv = short_conv(value_b.astype(jnp.float32), filter_b[2])
    product = key_conv * value_conv
    positions = jnp.arange(SEQ).astype(product.dtype)[:, None]

    def add_mode(index, kernel):
        mode_rate = rate_b[index]
        weight = residue_b[index] * jnp.sqrt(-jnp.expm1(-2.0 * mode_rate))
        return kernel + weight * jnp.exp(-mode_rate * positions)
    kernel = lax.fori_loop(0, ORDER, add_mode, jnp.zeros_like(product))
    spectrum = jnp.fft.rfft(product, n=2 * SEQ, axis=0) * jnp.fft.rfft(kernel, n=2 * SEQ, axis=0)
    long_conv = jnp.fft.irfft(spectrum, n=2 * SEQ, axis=0)[:SEQ].astype(product.dtype)
    gated = query_conv * (long_conv + skip_b * product)
    return gated.astype(jnp.bfloat16)

def reference(query_proj, key_proj, value_proj, short_filter, residues, decay, skip_gain, residual, norm_gain):
    block_width = min(D, 512)
    blocks = D // block_width

    def split_rows(array):
        return array.reshape(SEQ, blocks, block_width).transpose(1, 0, 2)
    filters = short_filter.reshape(3, SHORT, blocks, block_width).transpose(2, 0, 1, 3)
    residue_blocks = residues.reshape(ORDER, blocks, block_width).transpose(1, 0, 2)
    rate_blocks = decay.reshape(ORDER, blocks, block_width).transpose(1, 0, 2)
    skip_blocks = skip_gain.reshape(blocks, block_width)
    outputs = lax.map(channel_block, (split_rows(query_proj), split_rows(key_proj), split_rows(value_proj), filters, residue_blocks, rate_blocks, skip_blocks))
    mixed = outputs.transpose(1, 0, 2).reshape(SEQ, D)
    summed = residual.astype(jnp.float32) + lax.optimization_barrier(mixed).astype(jnp.float32)
    squares = lax.optimization_barrier(jnp.sum(summed * summed, axis=1, keepdims=True))
    normed = (summed * lax.rsqrt(squares / D + 1e-05) * norm_gain).astype(jnp.bfloat16)
    return (mixed, normed)
```

```python
import functools

import jax
import jax.numpy as jnp
from jax import lax
from jax.experimental import pallas as pl
from jax.experimental.pallas import tpu as pltpu
from jax.sharding import PartitionSpec as P

MESH = pl.DeviceIdType.MESH
F32 = jnp.float32
BF16 = jnp.bfloat16


def kernel(
    count, peers, wire,
    q_ref, k_ref, v_ref, filter_ref, residue_ref, decay_ref, skip_ref, residual_ref, gain_ref,
    mixed_ref, normed_ref,
    rows_x, taps, modes, pole, weight, prod, gate, local, mix, total,
    state, prefix, plane,
    halo_out, halo_in, x_out, x_in, y_out, y_in, z_out, z_in, sq_out, sq_in,
    halo_ss, halo_rs, x_ss, x_rs, y_ss, y_rs, z_ss, z_rs, sq_ss, sq_rs,
):
    row_count, channels = q_ref.shape
    tap_count = filter_ref.shape[1]
    order = decay_ref.shape[0]
    tiles = channels // 128
    sub = min(8, tiles)
    groups = tiles // sub
    blocks = row_count // 8
    pitch = tiles * 8
    me = lax.axis_index("context")
    side = lax.axis_index("tensor")
    x = lax.rem(me, 2)
    y = lax.rem(me // 2, 2)
    z = me // 4
    depth = count // 4
    x_peer = me + 1 - 2 * x
    y_peer = me + 2 - 4 * y
    has_prev, has_next = me > 0, me < count - 1
    has_down, has_up = z > 0, z < depth - 1

    barrier = pltpu.get_barrier_semaphore()

    def greet(context, tensor):
        pl.semaphore_signal(barrier, inc=1, device_id=(context, tensor), device_id_type=MESH)

    greet(x_peer, side)
    greet(y_peer, side)
    for shift in range(1, peers):
        greet(me, lax.rem(side + shift, peers))
    pl.when(has_prev)(lambda: greet(me - 1, side))
    pl.when(has_next)(lambda: greet(me + 1, side))
    pl.when(has_down)(lambda: greet(me - 4, side))
    pl.when(has_up)(lambda: greet(me + 4, side))
    met = (
        1 + peers + has_prev.astype(jnp.int32) + has_next.astype(jnp.int32)
        + has_down.astype(jnp.int32) + has_up.astype(jnp.int32)
    )

    inputs = (q_ref, k_ref, v_ref)
    span = sub * 8
    for group in range(groups):
        for i in range(3):
            for l in range(sub):
                lane = (group * sub + l) * 128
                last = inputs[i][row_count - 16 : row_count, lane : lane + 128].astype(F32)
                mix[(i * sub + l) * 8 : (i * sub + l + 1) * 8, :] = last[8:16]
        halo_out[group] = mix[0 : 3 * span, :].astype(BF16)

    pl.semaphore_wait(barrier, met)

    def halo_copy(group):
        return pltpu.make_async_remote_copy(
            src_ref=halo_out.at[group], dst_ref=halo_in.at[group],
            send_sem=halo_ss.at[group], recv_sem=halo_rs.at[group],
            device_id=(lax.rem(me + 1, count), side), device_id_type=MESH,
        )

    def x_copy(group):
        return pltpu.make_async_remote_copy(
            src_ref=x_out.at[group], dst_ref=x_in.at[group],
            send_sem=x_ss.at[group], recv_sem=x_rs.at[group],
            device_id=(x_peer, side), device_id_type=MESH,
        )

    def y_copy(group):
        return pltpu.make_async_remote_copy(
            src_ref=y_out.at[group], dst_ref=y_in.at[group],
            send_sem=y_ss.at[group], recv_sem=y_rs.at[group],
            device_id=(y_peer, side), device_id_type=MESH,
        )

    def z_copy(group):
        return pltpu.make_async_remote_copy(
            src_ref=z_out.at[group], dst_ref=z_in.at[group],
            send_sem=z_ss.at[group], recv_sem=z_rs.at[group],
            device_id=(lax.rem(me + 4, count), side), device_id_type=MESH,
        )

    def to_wire(value):
        return value.reshape(order * sub, 128).astype(BF16) if wire == BF16 else value

    def from_wire(value):
        return value.astype(F32).reshape(order, sub, 128) if wire == BF16 else value

    @pl.when(has_next)
    def _():
        for group in range(groups):
            halo_copy(group).start()

    for l in range(tiles):
        lane = l * 128
        for i in range(3):
            base = (i * tiles + l) * 8
            taps[base : base + tap_count, :] = filter_ref[i, :, lane : lane + 128]
        for part in range(order // 8):
            base = (part * tiles + l) * 8
            modes[0, base : base + 8, :] = decay_ref[part * 8 : part * 8 + 8, lane : lane + 128]
            modes[1, base : base + 8, :] = residue_ref[part * 8 : part * 8 + 8, lane : lane + 128]
    for group in range(groups):
        for m in range(order):
            start = ((m // 8) * tiles + group * sub) * 8 + m % 8
            rate = modes[0, pl.ds(start, sub, stride=8), :]
            residue = modes[1, pl.ds(start, sub, stride=8), :]
            pole[group, 0, m] = jnp.exp(-rate)
            pole[group, 1, m] = jnp.exp(-rate * float(row_count))
            pole[group, 2, m] = jnp.exp(-rate * float(row_count - 8))
            weight[group, m] = residue * jnp.sqrt(1.0 - jnp.exp(-2.0 * rate))

    def convolve(i, group, block):
        first = group * sub * 8
        f = [
            taps[pl.ds(i * pitch + first + j, sub, stride=8), :] for j in range(tap_count)
        ]
        rows = []
        for s in range(1 - tap_count, 8):
            start = (block + (1 if s >= 0 else 0)) * pitch + first + s % 8
            rows.append(rows_x[i, pl.ds(start, sub, stride=8), :])
        outs = []
        for r in range(8):
            acc = rows[r + tap_count - 1] * f[0]
            for j in range(1, tap_count):
                acc = acc + rows[r + tap_count - 1 - j] * f[j]
            outs.append(acc)
        return outs

    def convert(group):
        def body(pair, carry):
            for i in range(3):
                for l in range(sub):
                    tile = group * sub + l
                    at = pl.ds(pl.multiple_of(pair * 16, 16), 16)
                    value = inputs[i][at, tile * 128 : tile * 128 + 128].astype(F32)
                    for half in range(2):
                        start = (pair * 2 + half + 1) * pitch + tile * 8
                        start = pl.multiple_of(start, 8)
                        rows_x[i, pl.ds(start, 8), :] = value[half * 8 : half * 8 + 8]
            return carry

        lax.fori_loop(0, blocks // 2, body, 0)

    def scan_block(group, block, h):
        keys = convolve(1, group, block)
        values = convolve(2, group, block)
        a = pole[group, 0]
        for r in range(8):
            p = keys[r] * values[r]
            prod[block * 8 + r, group] = p
            h = a * h + p[None]
        return h

    zero_state = jnp.zeros((order, sub, 128), F32)

    def phase_a(group):
        convert(group)
        h = lax.fori_loop(1, blocks, lambda b, h: scan_block(group, b, h), zero_state)
        state[group] = h

        @pl.when(has_prev)
        def _():
            halo_copy(group).wait_recv()
            for i in range(3):
                rows_x[i, group * span : group * span + span, :] = halo_in[
                    group, i * span : (i + 1) * span, :
                ].astype(F32)

        @pl.when(jnp.logical_not(has_prev))
        def _():
            for i in range(3):
                rows_x[i, group * span : group * span + span, :] = jnp.zeros((span, 128), F32)

        first = scan_block(group, 0, zero_state)
        e = state[group] + pole[group, 2] * first
        state[group] = e
        x_out[group] = to_wire(e)
        x_copy(group).start()

    def stage_y(group):
        x_copy(group).wait_recv()
        other = from_wire(x_in[group])
        own = state[group]
        b = pole[group, 1]
        upper = x.astype(F32)
        both = jnp.where(x == 1, b * other + own, b * own + other)
        prefix[group] = other * upper
        plane[group] = both
        y_out[group] = to_wire(both)
        y_copy(group).start()

    def stage_z(group):
        y_copy(group).wait_recv()
        other = from_wire(y_in[group])
        own = plane[group]
        b = pole[group, 1]
        b2 = b * b
        all4 = jnp.where(y == 1, b2 * other + own, b2 * own + other)
        plane[group] = all4
        here = prefix[group]
        prefix[group] = jnp.where(y == 1, here + jnp.where(x == 1, b, 1.0) * other, here)

        @pl.when(jnp.logical_and(z == 0, has_up))
        def _():
            z_out[group] = to_wire(all4)
            z_copy(group).start()

    def stage_chain(group):
        @pl.when(has_down)
        def _():
            z_copy(group).wait_recv()
            other = from_wire(z_in[group])
            b = pole[group, 1]
            b2 = b * b

            @pl.when(has_up)
            def _():
                z_out[group] = to_wire(b2 * b2 * other + plane[group])
                z_copy(group).start()

            scale = jnp.where(x == 1, b, 1.0) * jnp.where(y == 1, b2, 1.0)
            prefix[group] = prefix[group] + scale * other

    def phase_b(group):
        def body(block, h):
            gates = convolve(0, group, block)
            a = pole[group, 0]
            w = weight[group]
            skip = skip_ref[group]
            for r in range(8):
                p = prod[block * 8 + r, group]
                h = a * h + p[None]
                local[block * 8 + r, group] = jnp.sum(w * h, axis=0) + skip * p
                gate[block * 8 + r, group] = gates[r]
            return h

        lax.fori_loop(0, blocks, body, zero_state)

    def phase_c(group):
        def body(block, g):
            a = pole[group, 0]
            for r in range(8):
                g = a * g
                value = gate[block * 8 + r, group] * (
                    local[block * 8 + r, group] + jnp.sum(g, axis=0)
                )
                start = block * pitch + group * span + r
                mix[pl.ds(start, sub, stride=8), :] = value
            return g

        lax.fori_loop(0, blocks, body, weight[group] * prefix[group])

    for step in range(groups + 3):
        if step < groups:
            phase_a(step)
        if 0 <= step - 1 < groups:
            stage_y(step - 1)
        if 0 <= step - 2 < groups:
            stage_z(step - 2)
        if 0 <= step - 3 < groups:
            phase_b(step - 3)
            stage_chain(step - 3)
    for group in range(groups):
        phase_c(group)

    def finish(pair, carry):
        at = pl.ds(pl.multiple_of(pair * 16, 16), 16)
        squares = jnp.zeros((16, 128), F32)
        for l in range(tiles):
            parts = []
            for half in range(2):
                start = pl.multiple_of((pair * 2 + half) * pitch + l * 8, 8)
                parts.append(mix[pl.ds(start, 8), :])
            rounded = jnp.concatenate(parts, axis=0).astype(BF16)
            lanes = slice(l * 128, l * 128 + 128)
            mixed_ref[at, lanes] = rounded
            summed = residual_ref[at, lanes].astype(F32) + rounded.astype(F32)
            total[at, lanes] = summed
            squares = squares + summed * summed
        sq_out[at, :] = squares
        return carry

    lax.fori_loop(0, blocks // 2, finish, 0)

    def sq_copy(shift):
        return pltpu.make_async_remote_copy(
            src_ref=sq_out, dst_ref=sq_in.at[shift - 1],
            send_sem=sq_ss.at[shift - 1], recv_sem=sq_rs.at[shift - 1],
            device_id=(me, lax.rem(side + shift, peers)), device_id_type=MESH,
        )

    for shift in range(1, peers):
        sq_copy(shift).start()
    for shift in range(1, peers):
        sq_copy(shift).wait_recv()

    def normalise(pair, carry):
        at = pl.ds(pl.multiple_of(pair * 16, 16), 16)
        squares = sq_out[at, :]
        for shift in range(1, peers):
            squares = squares + sq_in[shift - 1, at, :]
        mean = jnp.sum(squares, axis=1, keepdims=True) / float(channels * peers)
        scale = lax.rsqrt(mean + 1e-05)
        for l in range(tiles):
            lanes = slice(l * 128, l * 128 + 128)
            normed_ref[at, lanes] = (total[at, lanes] * scale * gain_ref[:, lanes]).astype(BF16)
        return carry

    lax.fori_loop(0, blocks // 2, normalise, 0)

    for shift in range(1, peers):
        sq_copy(shift).wait_send()
    for group in range(groups):
        x_copy(group).wait_send()
        y_copy(group).wait_send()

    @pl.when(has_next)
    def _():
        for group in range(groups):
            halo_copy(group).wait_send()

    @pl.when(has_up)
    def _():
        for group in range(groups):
            z_copy(group).wait_send()


def shards(
    count, peers,
    query_proj, key_proj, value_proj, short_filter, residues, decay, skip_gain, residual, norm_gain
):
    rows, channels = query_proj.shape
    order = decay.shape[0]
    tiles = channels // 128
    sub = min(8, tiles)
    groups = tiles // sub
    wire = BF16 if sub == 8 else F32
    packet = (groups, order * sub, 128) if wire == BF16 else (groups, order, sub, 128)
    modal = (groups, order, sub, 128)
    by_row = pltpu.VMEM((rows, groups, sub, 128), F32)
    dma = pltpu.SemaphoreType.DMA
    whole = pl.BlockSpec(memory_space=pltpu.VMEM)
    out = jax.ShapeDtypeStruct((rows, channels), BF16)
    return pl.pallas_call(
        functools.partial(kernel, count, peers, wire),
        out_shape=(out, out),
        in_specs=[whole] * 9,
        out_specs=(whole, whole),
        scratch_shapes=[
            pltpu.VMEM((3, (rows + 8) * tiles, 128), F32),
            pltpu.VMEM((3 * tiles * 8, 128), F32),
            pltpu.VMEM((2, order * tiles, 128), F32),
            pltpu.VMEM((groups, 3, order, sub, 128), F32),
            pltpu.VMEM(modal, F32),
            by_row, by_row, by_row,
            pltpu.VMEM((rows * tiles, 128), F32),
            pltpu.VMEM((rows, channels), F32),
            pltpu.VMEM(modal, F32), pltpu.VMEM(modal, F32), pltpu.VMEM(modal, F32),
            pltpu.VMEM((groups, 3 * sub * 8, 128), BF16),
            pltpu.VMEM((groups, 3 * sub * 8, 128), BF16),
            pltpu.VMEM(packet, wire), pltpu.VMEM(packet, wire),
            pltpu.VMEM(packet, wire), pltpu.VMEM(packet, wire),
            pltpu.VMEM(packet, wire), pltpu.VMEM(packet, wire),
            pltpu.VMEM((rows, 128), F32), pltpu.VMEM((max(1, peers - 1), rows, 128), F32),
            dma((groups,)), dma((groups,)), dma((groups,)), dma((groups,)),
            dma((groups,)), dma((groups,)), dma((groups,)), dma((groups,)),
            dma((max(1, peers - 1),)), dma((max(1, peers - 1),)),
        ],
        compiler_params=pltpu.CompilerParams(
            collective_id=0, has_side_effects=True, vmem_limit_bytes=50 * 1024 * 1024
        ),
    )(
        query_proj, key_proj, value_proj, short_filter, residues, decay,
        skip_gain.reshape(groups, sub, 128), residual, norm_gain.reshape(1, channels),
    )


def solution(mesh):
    in_specs = (
        P("context", "tensor"),
        P("context", "tensor"),
        P("context", "tensor"),
        P(None, None, "tensor"),
        P(None, "tensor"),
        P(None, "tensor"),
        P("tensor"),
        P("context", "tensor"),
        P("tensor"),
    )
    out_specs = (P("context", "tensor"), P("context", "tensor"))
    return jax.shard_map(
        functools.partial(shards, mesh.shape["context"], mesh.shape["tensor"]),
        mesh=mesh, in_specs=in_specs, out_specs=out_specs, check_vma=False,
    )
```

```python
import functools

import jax
import jax.numpy as jnp
from jax import lax
from jax.experimental import pallas as pl
from jax.experimental.pallas import tpu as pltpu
from jax.sharding import PartitionSpec as P

MESH = pl.DeviceIdType.MESH
F32 = jnp.float32
BF16 = jnp.bfloat16


def kernel(
    count, peers, wire,
    q_hbm, k_hbm, v_hbm, filter_hbm, residue_hbm, decay_hbm, skip_hbm, residual_hbm, gain_hbm,
    mixed_ref, normed_ref,
    inputs, filter_ref, residue_ref, decay_ref, skip_ref, residual_ref, gain_ref, edge,
    rows_x, taps, modes, pole, weight, table, direct, prod, gate, starts, mix, total,
    state, first_ref, prefix, plane, column,
    halo_out, halo_in, x_out, x_in, y_out, y_in, z_out, z_in, sq_out, sq_in,
    in_sem, par_sem, edge_sem,
    halo_ss, halo_rs, x_ss, x_rs, y_ss, y_rs, z_ss, z_rs, sq_ss, sq_rs,
):
    row_count, channels = q_hbm.shape
    tap_count = filter_hbm.shape[1]
    order = decay_hbm.shape[0]
    tiles = channels // 128
    sub = min(8, tiles)
    groups = tiles // sub
    blocks = row_count // 8
    pitch = tiles * 8
    span = sub * 8
    me = lax.axis_index("context")
    side = lax.axis_index("tensor")
    x = lax.rem(me, 2)
    y = lax.rem(me // 2, 2)
    z = me // 4
    depth = count // 4
    x_peer = me + 1 - 2 * x
    y_peer = me + 2 - 4 * y
    has_prev, has_next = me > 0, me < count - 1

    sources = (q_hbm, k_hbm, v_hbm)

    def edge_copy(i):
        return pltpu.make_async_copy(
            sources[i].at[row_count - 16 : row_count], edge.at[i], edge_sem.at[i]
        )

    def input_copy(i, group):
        lanes = slice(group * sub * 128, (group + 1) * sub * 128)
        return pltpu.make_async_copy(
            sources[i].at[:, lanes], inputs.at[i, :, lanes], in_sem.at[i, group]
        )

    params = (
        (decay_hbm, decay_ref), (residue_hbm, residue_ref), (filter_hbm, filter_ref),
        (skip_hbm, skip_ref), (gain_hbm, gain_ref), (residual_hbm, residual_ref),
    )

    def param_copy(i):
        return pltpu.make_async_copy(params[i][0], params[i][1], par_sem.at[i])

    for i in range(3):
        edge_copy(i).start()
    for i in range(3):
        param_copy(i).start()
    for group in range(groups):
        input_copy(1, group).start()
        input_copy(2, group).start()
    for group in range(groups):
        input_copy(0, group).start()
    for i in range(3, 6):
        param_copy(i).start()

    barrier = pltpu.get_barrier_semaphore()

    def greet(context, tensor):
        pl.semaphore_signal(barrier, inc=1, device_id=(context, tensor), device_id_type=MESH)

    greet(x_peer, side)
    greet(y_peer, side)
    for shift in range(1, peers):
        greet(me, lax.rem(side + shift, peers))
    pl.when(has_prev)(lambda: greet(me - 1, side))
    pl.when(has_next)(lambda: greet(me + 1, side))
    for shift in range(1, depth):
        greet(lax.rem(me + 4 * shift, count), side)
    met = peers + depth + has_prev.astype(jnp.int32) + has_next.astype(jnp.int32)

    for i in range(3):
        edge_copy(i).wait()
    for group in range(groups):
        for i in range(3):
            for l in range(sub):
                lane = (group * sub + l) * 128
                last = edge[i, :, lane : lane + 128].astype(F32)
                mix[(i * sub + l) * 8 : (i * sub + l + 1) * 8, :] = last[8:16]
        halo_out[group] = mix[0 : 3 * span, :].astype(BF16)

    pl.semaphore_wait(barrier, met)

    def remote(src, dst, send, recv, context, tensor=side):
        return pltpu.make_async_remote_copy(
            src_ref=src, dst_ref=dst, send_sem=send, recv_sem=recv,
            device_id=(context, tensor), device_id_type=MESH,
        )

    def halo_copy(group):
        return remote(
            halo_out.at[group], halo_in.at[group], halo_ss.at[group], halo_rs.at[group],
            lax.rem(me + 1, count),
        )

    def x_copy(group):
        return remote(x_out.at[group], x_in.at[group], x_ss.at[group], x_rs.at[group], x_peer)

    def y_copy(group):
        return remote(y_out.at[group], y_in.at[group], y_ss.at[group], y_rs.at[group], y_peer)

    def z_copy(group, shift):
        return remote(
            z_out.at[group], z_in.at[group, shift - 1],
            z_ss.at[group, shift - 1], z_rs.at[group, shift - 1],
            lax.rem(me + 4 * shift, count),
        )

    def to_wire(value):
        return value.reshape(order * sub, 128).astype(BF16) if wire == BF16 else value

    def from_wire(value):
        return value.astype(F32).reshape(order, sub, 128) if wire == BF16 else value

    @pl.when(has_next)
    def _():
        for group in range(groups):
            halo_copy(group).start()

    for i in range(3):
        param_copy(i).wait()
    for l in range(tiles):
        lane = l * 128
        for i in range(3):
            base = (i * tiles + l) * 8
            taps[base : base + tap_count, :] = filter_ref[i, :, lane : lane + 128]
        for part in range(order // 8):
            base = (part * tiles + l) * 8
            modes[0, base : base + 8, :] = decay_ref[part * 8 : part * 8 + 8, lane : lane + 128]
            modes[1, base : base + 8, :] = residue_ref[part * 8 : part * 8 + 8, lane : lane + 128]
    for group in range(groups):
        for m in range(order):
            start = ((m // 8) * tiles + group * sub) * 8 + m % 8
            rate = modes[0, pl.ds(start, sub, stride=8), :]
            residue = modes[1, pl.ds(start, sub, stride=8), :]
            pole[group, 0, m] = jnp.exp(-rate)
            pole[group, 1, m] = jnp.exp(-rate * float(row_count))
            pole[group, 2, m] = jnp.exp(-rate * float(row_count - 8))
            pole[group, 3, m] = jnp.exp(-rate * 8.0)
            weight[group, m] = residue * jnp.sqrt(1.0 - jnp.exp(-2.0 * rate))

    def convolve(i, group, block):
        first = group * sub * 8
        f = [
            taps[pl.ds(i * pitch + first + j, sub, stride=8), :] for j in range(tap_count)
        ]
        rows = []
        for s in range(1 - tap_count, 8):
            start = (block + (1 if s >= 0 else 0)) * pitch + first + s % 8
            rows.append(rows_x[i, pl.ds(start, sub, stride=8), :])
        outs = []
        for r in range(8):
            acc = rows[r + tap_count - 1] * f[0]
            for j in range(1, tap_count):
                acc = acc + rows[r + tap_count - 1 - j] * f[j]
            outs.append(acc)
        return outs

    def convert(chosen, group):
        for i in chosen:
            input_copy(i, group).wait()

        def body(pair, carry):
            for i in chosen:
                for l in range(sub):
                    tile = group * sub + l
                    at = pl.ds(pl.multiple_of(pair * 16, 16), 16)
                    value = inputs[i, at, tile * 128 : tile * 128 + 128].astype(F32)
                    for half in range(2):
                        start = (pair * 2 + half + 1) * pitch + tile * 8
                        start = pl.multiple_of(start, 8)
                        rows_x[i, pl.ds(start, 8), :] = value[half * 8 : half * 8 + 8]
            return carry

        lax.fori_loop(0, blocks // 2, body, 0)

    def place_halo(chosen, group):
        at = slice(group * span, group * span + span)

        @pl.when(has_prev)
        def _():
            for i in chosen:
                rows_x[i, at, :] = halo_in[group, i * span : (i + 1) * span, :].astype(F32)

        @pl.when(jnp.logical_not(has_prev))
        def _():
            for i in chosen:
                rows_x[i, at, :] = jnp.zeros((span, 128), F32)

    def scan_block(group, block, h):
        keys = convolve(1, group, block)
        values = convolve(2, group, block)
        a = pole[group, 0]
        for r in range(8):
            p = keys[r] * values[r]
            prod[block * 8 + r, group] = p
            h = a * h + p[None]
        return h

    zero_state = jnp.zeros((order, sub, 128), F32)

    def phase_a(group):
        convert((1, 2), group)

        def body(block, h):
            starts[group, block] = h
            return scan_block(group, block, h)

        h = lax.fori_loop(1, blocks, body, zero_state)
        state[group] = h
        pl.when(has_prev)(lambda: halo_copy(group).wait_recv())
        place_halo((1, 2), group)
        first = scan_block(group, 0, zero_state)
        first_ref[group] = first
        e = state[group] + pole[group, 2] * first
        state[group] = e
        x_out[group] = to_wire(e)
        x_copy(group).start()

    def stage_y(group):
        x_copy(group).wait_recv()
        other = from_wire(x_in[group])
        own = state[group]
        b = pole[group, 1]
        both = jnp.where(x == 1, b * other + own, b * own + other)
        prefix[group] = other * x.astype(F32)
        plane[group] = both
        y_out[group] = to_wire(both)
        y_copy(group).start()

    def stage_z(group):
        y_copy(group).wait_recv()
        other = from_wire(y_in[group])
        own = plane[group]
        b = pole[group, 1]
        b2 = b * b
        all4 = jnp.where(y == 1, b2 * other + own, b2 * own + other)
        here = prefix[group]
        prefix[group] = jnp.where(y == 1, here + jnp.where(x == 1, b, 1.0) * other, here)
        z_out[group] = to_wire(all4)
        for shift in range(1, depth):
            pl.when(z + shift < depth)(lambda shift=shift: z_copy(group, shift).start())

    def stage_end(group):
        b = pole[group, 1]
        b2 = b * b
        b4 = b2 * b2
        column[...] = zero_state
        for shift in range(depth - 1, 0, -1):

            @pl.when(z >= shift)
            def _(shift=shift):
                z_copy(group, shift).wait_recv()
                column[...] = b4 * column[...] + from_wire(z_in[group, shift - 1])

        scale = jnp.where(x == 1, b, 1.0) * jnp.where(y == 1, b2, 1.0)
        prefix[group] = prefix[group] + scale * column[...]

    def phase_b(group):
        convert((0,), group)
        place_halo((0,), group)

        def body(block, carry):
            gates = convolve(0, group, block)
            for r in range(8):
                gate[block * 8 + r, group] = gates[r]
            return carry

        lax.fori_loop(0, blocks, body, 0)
        a = pole[group, 0]
        w = weight[group]
        direct[group, 0] = jnp.sum(w, axis=0) + skip_ref[group]
        for r in range(8):
            w = w * a
            table[group, r] = w
            if r < 7:
                direct[group, r + 1] = jnp.sum(w, axis=0)

    def phase_c(group):
        def emit(block, s):
            p = [prod[block * 8 + r, group] for r in range(8)]
            for r in range(8):
                value = jnp.sum(table[group, r] * s, axis=0)
                near = direct[group, 0] * p[r]
                for j in range(1, r + 1):
                    near = near + direct[group, j] * p[r - j]
                start = block * pitch + group * span + r
                mix[pl.ds(start, sub, stride=8), :] = gate[block * 8 + r, group] * (value + near)

        a8 = pole[group, 3]
        s = prefix[group]
        emit(0, s)

        def body(block, s):
            emit(block, s + starts[group, block])
            return pole[group, 3] * s

        lax.fori_loop(1, blocks, body, a8 * s + first_ref[group])

    for step in range(groups + 2):
        if step < groups:
            phase_a(step)
        if 0 <= step - 1 < groups:
            stage_y(step - 1)
        if 0 <= step - 2 < groups:
            stage_z(step - 2)
        if step == groups - 1:
            param_copy(3).wait()
            for group in range(0, groups, 3):
                phase_b(group)
        if step >= groups:
            for group in range(step - groups + 1, groups, 3):
                phase_b(group)
    for group in range(groups):
        stage_end(group)
        phase_c(group)

    param_copy(4).wait()
    param_copy(5).wait()

    def finish(pair, carry):
        at = pl.ds(pl.multiple_of(pair * 16, 16), 16)
        squares = jnp.zeros((16, 128), F32)
        for l in range(tiles):
            parts = []
            for half in range(2):
                start = pl.multiple_of((pair * 2 + half) * pitch + l * 8, 8)
                parts.append(mix[pl.ds(start, 8), :])
            rounded = jnp.concatenate(parts, axis=0).astype(BF16)
            lanes = slice(l * 128, l * 128 + 128)
            mixed_ref[at, lanes] = rounded
            summed = residual_ref[at, lanes].astype(F32) + rounded.astype(F32)
            total[at, lanes] = summed
            squares = squares + summed * summed
        sq_out[at, :] = squares
        return carry

    lax.fori_loop(0, blocks // 2, finish, 0)

    def sq_copy(shift):
        return remote(
            sq_out, sq_in.at[shift - 1], sq_ss.at[shift - 1], sq_rs.at[shift - 1],
            me, lax.rem(side + shift, peers),
        )

    for shift in range(1, peers):
        sq_copy(shift).start()
    for shift in range(1, peers):
        sq_copy(shift).wait_recv()

    def normalise(pair, carry):
        at = pl.ds(pl.multiple_of(pair * 16, 16), 16)
        squares = sq_out[at, :]
        for shift in range(1, peers):
            squares = squares + sq_in[shift - 1, at, :]
        mean = jnp.sum(squares, axis=1, keepdims=True) / float(channels * peers)
        scale = lax.rsqrt(mean + 1e-05)
        for l in range(tiles):
            lanes = slice(l * 128, l * 128 + 128)
            normed_ref[at, lanes] = (total[at, lanes] * scale * gain_ref[:, lanes]).astype(BF16)
        return carry

    lax.fori_loop(0, blocks // 2, normalise, 0)

    for shift in range(1, peers):
        sq_copy(shift).wait_send()
    for group in range(groups):
        x_copy(group).wait_send()
        y_copy(group).wait_send()
        for shift in range(1, depth):
            pl.when(z + shift < depth)(
                lambda group=group, shift=shift: z_copy(group, shift).wait_send()
            )

    @pl.when(has_next)
    def _():
        for group in range(groups):
            halo_copy(group).wait_send()


def shards(
    count, peers,
    query_proj, key_proj, value_proj, short_filter, residues, decay, skip_gain, residual, norm_gain
):
    rows, channels = query_proj.shape
    order = decay.shape[0]
    tap_count = short_filter.shape[1]
    tiles = channels // 128
    sub = min(8, tiles)
    groups = tiles // sub
    depth = count // 4
    wire = BF16 if sub == 8 else F32
    packet = (order * sub, 128) if wire == BF16 else (order, sub, 128)
    others = max(1, peers - 1)
    packets = pltpu.VMEM((groups, *packet), wire)
    modal = pltpu.VMEM((groups, order, sub, 128), F32)
    by_row = pltpu.VMEM((rows, groups, sub, 128), F32)
    dma = pltpu.SemaphoreType.DMA
    hbm = pl.BlockSpec(memory_space=pltpu.HBM)
    whole = pl.BlockSpec(memory_space=pltpu.VMEM)
    out = jax.ShapeDtypeStruct((rows, channels), BF16)
    return pl.pallas_call(
        functools.partial(kernel, count, peers, wire),
        out_shape=(out, out),
        in_specs=[hbm] * 9,
        out_specs=(whole, whole),
        scratch_shapes=[
            pltpu.VMEM((3, rows, channels), BF16),
            pltpu.VMEM((3, tap_count, channels), F32),
            pltpu.VMEM((order, channels), F32),
            pltpu.VMEM((order, channels), F32),
            pltpu.VMEM((groups, sub, 128), F32),
            pltpu.VMEM((rows, channels), BF16),
            pltpu.VMEM((1, channels), F32),
            pltpu.VMEM((3, 16, channels), BF16),
            pltpu.VMEM((3, (rows + 8) * tiles, 128), F32),
            pltpu.VMEM((3 * tiles * 8, 128), F32),
            pltpu.VMEM((2, order * tiles, 128), F32),
            pltpu.VMEM((groups, 4, order, sub, 128), F32),
            modal,
            pltpu.VMEM((groups, 8, order, sub, 128), F32),
            pltpu.VMEM((groups, 8, sub, 128), F32),
            by_row, by_row,
            pltpu.VMEM((groups, rows // 8, order, sub, 128), F32),
            pltpu.VMEM((rows * tiles, 128), F32),
            pltpu.VMEM((rows, channels), F32),
            modal, modal, modal, modal,
            pltpu.VMEM((order, sub, 128), F32),
            pltpu.VMEM((groups, 3 * sub * 8, 128), BF16),
            pltpu.VMEM((groups, 3 * sub * 8, 128), BF16),
            packets, packets, packets, packets, packets,
            pltpu.VMEM((groups, depth - 1, *packet), wire),
            pltpu.VMEM((rows, 128), F32), pltpu.VMEM((others, rows, 128), F32),
            dma((3, groups)), dma((6,)), dma((3,)),
            dma((groups,)), dma((groups,)), dma((groups,)), dma((groups,)),
            dma((groups,)), dma((groups,)), dma((groups, depth - 1)), dma((groups, depth - 1)),
            dma((others,)), dma((others,)),
        ],
        compiler_params=pltpu.CompilerParams(
            collective_id=0, has_side_effects=True, vmem_limit_bytes=60 * 1024 * 1024
        ),
    )(
        query_proj, key_proj, value_proj, short_filter, residues, decay,
        skip_gain.reshape(groups, sub, 128), residual, norm_gain.reshape(1, channels),
    )


def solution(mesh):
    in_specs = (
        P("context", "tensor"),
        P("context", "tensor"),
        P("context", "tensor"),
        P(None, None, "tensor"),
        P(None, "tensor"),
        P(None, "tensor"),
        P("tensor"),
        P("context", "tensor"),
        P("tensor"),
    )
    out_specs = (P("context", "tensor"), P("context", "tensor"))
    return jax.shard_map(
        functools.partial(shards, mesh.shape["context"], mesh.shape["tensor"]),
        mesh=mesh, in_specs=in_specs, out_specs=out_specs, check_vma=False,
    )
```

```python
import functools

import jax
import jax.numpy as jnp
from jax import lax
from jax.experimental import pallas as pl
from jax.experimental.pallas import tpu as pltpu
from jax.sharding import PartitionSpec as P

MESH = pl.DeviceIdType.MESH
F32 = jnp.float32
BF16 = jnp.bfloat16


def kernel(
    count, peers, wire,
    q_hbm, k_hbm, v_hbm, filter_hbm, residue_hbm, decay_hbm, skip_hbm, residual_hbm,
    mixed_hbm, squares_ref,
    inputs, filter_ref, residue_ref, decay_ref, skip_ref, residual_ref, edge,
    rows_x, turn, taps, taps_raw, modes, pole, weight, table, direct, prod, gate, starts, mix, mixed,
    state, first_ref, prefix, plane, column,
    halo_out, halo_in, x_out, x_in, y_out, y_in, z_out, z_in, sq_out, sq_in,
    in_sem, par_sem, edge_sem, out_sem,
    halo_ss, halo_rs, x_ss, x_rs, y_ss, y_rs, z_ss, z_rs, sq_ss, sq_rs,
):
    row_count, channels = q_hbm.shape
    tap_count = filter_hbm.shape[1]
    order = decay_hbm.shape[0]
    tiles = channels // 128
    sub = min(8, tiles)
    groups = tiles // sub
    blocks = row_count // 8
    pitch = tiles * 8
    span = sub * 8
    me = lax.axis_index("context")
    side = lax.axis_index("tensor")
    x = lax.rem(me, 2)
    y = lax.rem(me // 2, 2)
    z = me // 4
    depth = count // 4
    x_peer = me + 1 - 2 * x
    y_peer = me + 2 - 4 * y
    has_prev, has_next = me > 0, me < count - 1

    sources = (q_hbm, k_hbm, v_hbm)

    def edge_copy(i):
        return pltpu.make_async_copy(
            sources[i].at[row_count - 16 : row_count], edge.at[i], edge_sem.at[i]
        )

    def input_copy(i, group):
        lanes = slice(group * sub * 128, (group + 1) * sub * 128)
        return pltpu.make_async_copy(
            sources[i].at[:, lanes], inputs.at[i, :, lanes], in_sem.at[i, group]
        )

    params = (
        (decay_hbm, decay_ref), (residue_hbm, residue_ref), (filter_hbm, filter_ref),
        (skip_hbm, skip_ref), (residual_hbm, residual_ref),
    )

    def param_copy(i):
        return pltpu.make_async_copy(params[i][0], params[i][1], par_sem.at[i])

    for i in range(3):
        edge_copy(i).start()
    for i in range(3):
        param_copy(i).start()
    for group in range(groups):
        input_copy(1, group).start()
        input_copy(2, group).start()
    for group in range(groups):
        input_copy(0, group).start()
    for i in range(3, 5):
        param_copy(i).start()

    barrier = pltpu.get_barrier_semaphore()

    def greet(context, tensor):
        pl.semaphore_signal(barrier, inc=1, device_id=(context, tensor), device_id_type=MESH)

    greet(x_peer, side)
    greet(y_peer, side)
    for shift in range(1, peers):
        greet(me, lax.rem(side + shift, peers))
    pl.when(has_prev)(lambda: greet(me - 1, side))
    pl.when(has_next)(lambda: greet(me + 1, side))
    for shift in range(1, depth):
        greet(lax.rem(me + 4 * shift, count), side)
    met = peers + depth + has_prev.astype(jnp.int32) + has_next.astype(jnp.int32)

    for i in range(3):
        edge_copy(i).wait()
    for group in range(groups):
        for i in range(3):
            for l in range(sub):
                lane = (group * sub + l) * 128
                last = edge[i, :, lane : lane + 128].astype(F32)
                mix[(i * sub + l) * 8 : (i * sub + l + 1) * 8, :] = last[8:16]
        halo_out[group] = mix[0 : 3 * span, :].astype(BF16)

    pl.semaphore_wait(barrier, met)

    def remote(src, dst, send, recv, context, tensor=side):
        return pltpu.make_async_remote_copy(
            src_ref=src, dst_ref=dst, send_sem=send, recv_sem=recv,
            device_id=(context, tensor), device_id_type=MESH,
        )

    def halo_copy(group):
        return remote(
            halo_out.at[group], halo_in.at[group], halo_ss.at[group], halo_rs.at[group],
            lax.rem(me + 1, count),
        )

    def x_copy(group):
        return remote(x_out.at[group], x_in.at[group], x_ss.at[group], x_rs.at[group], x_peer)

    def y_copy(group):
        return remote(y_out.at[group], y_in.at[group], y_ss.at[group], y_rs.at[group], y_peer)

    def z_copy(group, shift):
        return remote(
            z_out.at[group], z_in.at[group, shift - 1],
            z_ss.at[group, shift - 1], z_rs.at[group, shift - 1],
            lax.rem(me + 4 * shift, count),
        )

    def to_wire(value):
        return value.reshape(order * sub, 128).astype(BF16) if wire == BF16 else value

    def from_wire(value):
        return value.astype(F32).reshape(order, sub, 128) if wire == BF16 else value

    @pl.when(has_next)
    def _():
        for group in range(groups):
            halo_copy(group).start()

    for i in range(3):
        param_copy(i).wait()
    for l in range(tiles):
        lane = l * 128
        for i in range(3):
            base = (i * tiles + l) * 8
            taps_raw[base : base + tap_count, :] = filter_ref[i, :, lane : lane + 128]
        for part in range(order // 8):
            base = (part * tiles + l) * 8
            modes[0, base : base + 8, :] = decay_ref[part * 8 : part * 8 + 8, lane : lane + 128]
            modes[1, base : base + 8, :] = residue_ref[part * 8 : part * 8 + 8, lane : lane + 128]
    for group in range(groups):
        for i in range(3):
            for j in range(tap_count):
                start = i * pitch + group * span + j
                taps[group, i, j] = taps_raw[pl.ds(start, sub, stride=8), :]
        for m in range(order):
            start = ((m // 8) * tiles + group * sub) * 8 + m % 8
            rate = modes[0, pl.ds(start, sub, stride=8), :]
            residue = modes[1, pl.ds(start, sub, stride=8), :]
            pole[group, 0, m] = jnp.exp(-rate)
            pole[group, 1, m] = jnp.exp(-rate * float(row_count))
            pole[group, 2, m] = jnp.exp(-rate * float(row_count - 8))
            pole[group, 3, m] = jnp.exp(-rate * 8.0)
            weight[group, m] = residue * jnp.sqrt(1.0 - jnp.exp(-2.0 * rate))

    def convolve(i, group, block):
        f = [taps[group, i, j] for j in range(tap_count)]
        rows = [rows_x[i, group, block * 8 + 8 + r] for r in range(1 - tap_count, 8)]
        outs = []
        for r in range(8):
            acc = rows[r + tap_count - 1] * f[0]
            for j in range(1, tap_count):
                acc = acc + rows[r + tap_count - 1 - j] * f[j]
            outs.append(acc)
        return outs

    def convert(chosen, group):
        for i in chosen:
            input_copy(i, group).wait()

        def body(pair, carry):
            at = pl.ds(pl.multiple_of(pair * 16, 16), 16)
            for i in chosen:
                for l in range(sub):
                    tile = group * sub + l
                    value = inputs[i, at, tile * 128 : tile * 128 + 128].astype(F32)
                    for half in range(2):
                        start = half * span + l * 8
                        turn[i, start : start + 8, :] = value[half * 8 : half * 8 + 8]
            for i in chosen:
                for r in range(16):
                    start = (r // 8) * span + r % 8
                    rows_x[i, group, pair * 16 + 8 + r] = turn[i, pl.ds(start, sub, stride=8), :]
            return carry

        lax.fori_loop(0, blocks // 2, body, 0)

    def place_halo(chosen, group):
        @pl.when(has_prev)
        def _():
            for i in chosen:
                turn[i, 0:span, :] = halo_in[group, i * span : (i + 1) * span, :].astype(F32)
            for i in chosen:
                for r in range(8):
                    rows_x[i, group, r] = turn[i, pl.ds(r, sub, stride=8), :]

        @pl.when(jnp.logical_not(has_prev))
        def _():
            for i in chosen:
                rows_x[i, group, 0:8] = jnp.zeros((8, sub, 128), F32)

    def scan_block(group, block, h):
        keys = convolve(1, group, block)
        values = convolve(2, group, block)
        a = pole[group, 0]
        for r in range(8):
            p = keys[r] * values[r]
            prod[block * 8 + r, group] = p
            h = a * h + p[None]
        return h

    zero_state = jnp.zeros((order, sub, 128), F32)

    def phase_a(group):
        convert((1, 2), group)

        def body(block, h):
            starts[group, block] = h
            return scan_block(group, block, h)

        h = lax.fori_loop(1, blocks, body, zero_state)
        state[group] = h
        pl.when(has_prev)(lambda: halo_copy(group).wait_recv())
        place_halo((1, 2), group)
        first = scan_block(group, 0, zero_state)
        first_ref[group] = first
        e = state[group] + pole[group, 2] * first
        state[group] = e
        x_out[group] = to_wire(e)
        x_copy(group).start()

    def stage_y(group):
        x_copy(group).wait_recv()
        other = from_wire(x_in[group])
        own = state[group]
        b = pole[group, 1]
        both = jnp.where(x == 1, b * other + own, b * own + other)
        prefix[group] = other * x.astype(F32)
        plane[group] = both
        y_out[group] = to_wire(both)
        y_copy(group).start()

    def stage_z(group):
        y_copy(group).wait_recv()
        other = from_wire(y_in[group])
        own = plane[group]
        b = pole[group, 1]
        b2 = b * b
        all4 = jnp.where(y == 1, b2 * other + own, b2 * own + other)
        here = prefix[group]
        prefix[group] = jnp.where(y == 1, here + jnp.where(x == 1, b, 1.0) * other, here)
        z_out[group] = to_wire(all4)
        for shift in range(1, depth):
            pl.when(z + shift < depth)(lambda shift=shift: z_copy(group, shift).start())

    def stage_end(group):
        b = pole[group, 1]
        b2 = b * b
        b4 = b2 * b2
        column[...] = zero_state
        for shift in range(depth - 1, 0, -1):

            @pl.when(z >= shift)
            def _(shift=shift):
                z_copy(group, shift).wait_recv()
                column[...] = b4 * column[...] + from_wire(z_in[group, shift - 1])

        scale = jnp.where(x == 1, b, 1.0) * jnp.where(y == 1, b2, 1.0)
        prefix[group] = prefix[group] + scale * column[...]

    def phase_b(group):
        convert((0,), group)
        place_halo((0,), group)

        def body(block, carry):
            gates = convolve(0, group, block)
            for r in range(8):
                gate[block * 8 + r, group] = gates[r]
            return carry

        lax.fori_loop(0, blocks, body, 0)
        a = pole[group, 0]
        w = weight[group]
        direct[group, 0] = jnp.sum(w, axis=0) + skip_ref[group]
        for r in range(8):
            w = w * a
            table[group, r] = w
            if r < 7:
                direct[group, r + 1] = jnp.sum(w, axis=0)

    def phase_c(group):
        def emit(block, s):
            p = [prod[block * 8 + r, group] for r in range(8)]
            for r in range(8):
                value = jnp.sum(table[group, r] * s, axis=0)
                near = direct[group, 0] * p[r]
                for j in range(1, r + 1):
                    near = near + direct[group, j] * p[r - j]
                start = block * pitch + group * span + r
                mix[pl.ds(start, sub, stride=8), :] = gate[block * 8 + r, group] * (value + near)

        a8 = pole[group, 3]
        s = prefix[group]
        emit(0, s)

        def body(block, s):
            emit(block, s + starts[group, block])
            return pole[group, 3] * s

        lax.fori_loop(1, blocks, body, a8 * s + first_ref[group])

    for step in range(groups + 2):
        if step < groups:
            phase_a(step)
        if 0 <= step - 1 < groups:
            stage_y(step - 1)
        if 0 <= step - 2 < groups:
            stage_z(step - 2)
        if step == groups - 1:
            param_copy(3).wait()
            for group in range(0, groups, 3):
                phase_b(group)
        if step >= groups:
            for group in range(step - groups + 1, groups, 3):
                phase_b(group)
    for group in range(groups):
        stage_end(group)
        phase_c(group)

    param_copy(4).wait()

    def out_copy(pair):
        at = pl.ds(pl.multiple_of(pair * 16, 16), 16)
        return pltpu.make_async_copy(mixed.at[at], mixed_hbm.at[at], out_sem.at[pair])

    def finish(pair, carry):
        at = pl.ds(pl.multiple_of(pair * 16, 16), 16)
        squares = jnp.zeros((16, 128), F32)
        for l in range(tiles):
            parts = []
            for half in range(2):
                start = pl.multiple_of((pair * 2 + half) * pitch + l * 8, 8)
                parts.append(mix[pl.ds(start, 8), :])
            rounded = jnp.concatenate(parts, axis=0).astype(BF16)
            lanes = slice(l * 128, l * 128 + 128)
            mixed[at, lanes] = rounded
            summed = residual_ref[at, lanes].astype(F32) + rounded.astype(F32)
            squares = squares + summed * summed
        sq_out[at, :] = squares
        out_copy(pair).start()
        return carry

    lax.fori_loop(0, blocks // 2, finish, 0)

    def sq_copy(shift):
        return remote(
            sq_out, sq_in.at[shift - 1], sq_ss.at[shift - 1], sq_rs.at[shift - 1],
            me, lax.rem(side + shift, peers),
        )

    for shift in range(1, peers):
        sq_copy(shift).start()
    for shift in range(1, peers):
        sq_copy(shift).wait_recv()

    squares = sq_out[...]
    for shift in range(1, peers):
        squares = squares + sq_in[shift - 1]
    squares_ref[...] = squares

    def drain(pair, carry):
        out_copy(pair).wait()
        return carry

    lax.fori_loop(0, blocks // 2, drain, 0)
    for shift in range(1, peers):
        sq_copy(shift).wait_send()
    for group in range(groups):
        x_copy(group).wait_send()
        y_copy(group).wait_send()
        for shift in range(1, depth):
            pl.when(z + shift < depth)(
                lambda group=group, shift=shift: z_copy(group, shift).wait_send()
            )

    @pl.when(has_next)
    def _():
        for group in range(groups):
            halo_copy(group).wait_send()


def normalise(
    width, mixed_hbm, residual_hbm, squares_ref, gain_ref, out_hbm, normed_hbm,
    mixed, residual, normed, mixed_sem, residual_sem, out_sem, normed_sem,
):
    row_count, channels = mixed_hbm.shape
    tall = 32
    pieces = row_count // tall

    ends = (
        (mixed_hbm, mixed, mixed_sem), (residual_hbm, residual, residual_sem),
        (mixed, out_hbm, out_sem), (normed, normed_hbm, normed_sem),
    )

    def copy(kind, piece):
        source, target, sems = ends[kind]
        at = slice(piece * tall, piece * tall + tall)
        return pltpu.make_async_copy(source.at[at], target.at[at], sems.at[piece])

    for piece in range(pieces):
        copy(0, piece).start()
        copy(1, piece).start()
    for piece in range(pieces):
        copy(0, piece).wait()
        copy(2, piece).start()
        copy(1, piece).wait()
        for part in range(tall // 16):
            at = slice(piece * tall + part * 16, piece * tall + part * 16 + 16)
            mean = jnp.sum(squares_ref[at, :], axis=1, keepdims=True) / float(width)
            scale = lax.rsqrt(mean + 1e-05)
            for l in range(channels // 128):
                lanes = slice(l * 128, l * 128 + 128)
                summed = residual[at, lanes].astype(F32) + mixed[at, lanes].astype(F32)
                normed[at, lanes] = (summed * scale * gain_ref[:, lanes]).astype(BF16)
        copy(3, piece).start()
    for piece in range(pieces):
        copy(2, piece).wait()
        copy(3, piece).wait()


def shards(
    count, peers,
    query_proj, key_proj, value_proj, short_filter, residues, decay, skip_gain, residual, norm_gain
):
    rows, channels = query_proj.shape
    order = decay.shape[0]
    tap_count = short_filter.shape[1]
    tiles = channels // 128
    sub = min(8, tiles)
    groups = tiles // sub
    depth = count // 4
    wire = BF16 if sub == 8 else F32
    packet = (order * sub, 128) if wire == BF16 else (order, sub, 128)
    others = max(1, peers - 1)
    packets = pltpu.VMEM((groups, *packet), wire)
    modal = pltpu.VMEM((groups, order, sub, 128), F32)
    by_row = pltpu.VMEM((rows, groups, sub, 128), F32)
    dma = pltpu.SemaphoreType.DMA
    hbm = pl.BlockSpec(memory_space=pltpu.HBM)
    whole = pl.BlockSpec(memory_space=pltpu.VMEM)
    out = jax.ShapeDtypeStruct((rows, channels), BF16)
    mixed, squares = pl.pallas_call(
        functools.partial(kernel, count, peers, wire),
        out_shape=(out, jax.ShapeDtypeStruct((rows, 128), F32)),
        in_specs=[hbm] * 8,
        out_specs=(hbm, whole),
        scratch_shapes=[
            pltpu.VMEM((3, rows, channels), BF16),
            pltpu.VMEM((3, tap_count, channels), F32),
            pltpu.VMEM((order, channels), F32),
            pltpu.VMEM((order, channels), F32),
            pltpu.VMEM((groups, sub, 128), F32),
            pltpu.VMEM((rows, channels), BF16),
            pltpu.VMEM((3, 16, channels), BF16),
            pltpu.VMEM((3, groups, rows + 8, sub, 128), F32),
            pltpu.VMEM((3, 16 * sub, 128), F32),
            pltpu.VMEM((groups, 3, tap_count, sub, 128), F32),
            pltpu.VMEM((3 * tiles * 8, 128), F32),
            pltpu.VMEM((2, order * tiles, 128), F32),
            pltpu.VMEM((groups, 4, order, sub, 128), F32),
            modal,
            pltpu.VMEM((groups, 8, order, sub, 128), F32),
            pltpu.VMEM((groups, 8, sub, 128), F32),
            by_row, by_row,
            pltpu.VMEM((groups, rows // 8, order, sub, 128), F32),
            pltpu.VMEM((rows * tiles, 128), F32),
            pltpu.VMEM((rows, channels), BF16),
            modal, modal, modal, modal,
            pltpu.VMEM((order, sub, 128), F32),
            pltpu.VMEM((groups, 3 * sub * 8, 128), BF16),
            pltpu.VMEM((groups, 3 * sub * 8, 128), BF16),
            packets, packets, packets, packets, packets,
            pltpu.VMEM((groups, depth - 1, *packet), wire),
            pltpu.VMEM((rows, 128), F32), pltpu.VMEM((others, rows, 128), F32),
            dma((3, groups)), dma((5,)), dma((3,)), dma((rows // 16,)),
            dma((groups,)), dma((groups,)), dma((groups,)), dma((groups,)),
            dma((groups,)), dma((groups,)), dma((groups, depth - 1)), dma((groups, depth - 1)),
            dma((others,)), dma((others,)),
        ],
        compiler_params=pltpu.CompilerParams(
            collective_id=0, has_side_effects=True, vmem_limit_bytes=60 * 1024 * 1024
        ),
    )(
        query_proj, key_proj, value_proj, short_filter, residues, decay,
        skip_gain.reshape(groups, sub, 128), residual,
    )
    pieces = rows // 32
    block = pltpu.VMEM((rows, channels), BF16)
    return pl.pallas_call(
        functools.partial(normalise, channels * peers),
        out_shape=(out, out),
        in_specs=[hbm, hbm, whole, whole],
        out_specs=(hbm, hbm),
        scratch_shapes=[
            block, block, block, dma((pieces,)), dma((pieces,)), dma((pieces,)), dma((pieces,))
        ],
        compiler_params=pltpu.CompilerParams(vmem_limit_bytes=60 * 1024 * 1024),
    )(mixed, residual, squares, norm_gain.reshape(1, channels))


def solution(mesh):
    in_specs = (
        P("context", "tensor"),
        P("context", "tensor"),
        P("context", "tensor"),
        P(None, None, "tensor"),
        P(None, "tensor"),
        P(None, "tensor"),
        P("tensor"),
        P("context", "tensor"),
        P("tensor"),
    )
    out_specs = (P("context", "tensor"), P("context", "tensor"))
    return jax.shard_map(
        functools.partial(shards, mesh.shape["context"], mesh.shape["tensor"]),
        mesh=mesh, in_specs=in_specs, out_specs=out_specs, check_vma=False,
    )
```

```python
import functools

import jax
import jax.numpy as jnp
from jax import lax
from jax.experimental import pallas as pl
from jax.experimental.pallas import tpu as pltpu
from jax.sharding import PartitionSpec as P

MESH = pl.DeviceIdType.MESH
F32 = jnp.float32
BF16 = jnp.bfloat16


def kernel(
    count, peers, wire,
    q_hbm, k_hbm, v_hbm, filter_hbm, residue_hbm, decay_hbm, skip_hbm, residual_hbm,
    mixed_hbm, squares_ref,
    inputs, filter_ref, residue_ref, decay_ref, skip_ref, residual_ref, edge,
    rows_x, turn, taps, taps_raw, modes, pole, weight, table, direct, prod, gate, starts, mix, mixed,
    state, first_ref, prefix, plane, column,
    halo_out, halo_in, x_out, x_in, y_out, y_in, z_out, z_in, sq_out, sq_in,
    in_sem, par_sem, edge_sem, out_sem,
    halo_ss, halo_rs, x_ss, x_rs, y_ss, y_rs, z_ss, z_rs, sq_ss, sq_rs,
):
    row_count, channels = q_hbm.shape
    tap_count = filter_hbm.shape[1]
    order = decay_hbm.shape[0]
    tiles = channels // 128
    sub = min(8, tiles)
    groups = tiles // sub
    blocks = row_count // 8
    pitch = tiles * 8
    span = sub * 8
    me = lax.axis_index("context")
    side = lax.axis_index("tensor")
    x = lax.rem(me, 2)
    y = lax.rem(me // 2, 2)
    z = me // 4
    depth = count // 4
    x_peer = me + 1 - 2 * x
    y_peer = me + 2 - 4 * y
    has_prev, has_next = me > 0, me < count - 1

    sources = (q_hbm, k_hbm, v_hbm)

    def edge_copy(i):
        return pltpu.make_async_copy(
            sources[i].at[row_count - 16 : row_count], edge.at[i], edge_sem.at[i]
        )

    def input_copy(i, group):
        lanes = pl.ds(pl.multiple_of(group * sub * 128, 128), sub * 128)
        return pltpu.make_async_copy(
            sources[i].at[:, lanes], inputs.at[i, :, lanes], in_sem.at[i, group]
        )

    params = (
        (decay_hbm, decay_ref), (residue_hbm, residue_ref), (filter_hbm, filter_ref),
        (skip_hbm, skip_ref), (residual_hbm, residual_ref),
    )

    def param_copy(i):
        return pltpu.make_async_copy(params[i][0], params[i][1], par_sem.at[i])

    for i in range(3):
        edge_copy(i).start()
    for i in range(3):
        param_copy(i).start()
    for group in range(groups):
        input_copy(1, group).start()
        input_copy(2, group).start()
    for group in range(groups):
        input_copy(0, group).start()
    for i in range(3, 5):
        param_copy(i).start()

    barrier = pltpu.get_barrier_semaphore()

    def greet(context, tensor):
        pl.semaphore_signal(barrier, inc=1, device_id=(context, tensor), device_id_type=MESH)

    greet(x_peer, side)
    greet(y_peer, side)
    for shift in range(1, peers):
        greet(me, lax.rem(side + shift, peers))
    pl.when(has_prev)(lambda: greet(me - 1, side))
    pl.when(has_next)(lambda: greet(me + 1, side))
    for shift in range(1, depth):
        greet(lax.rem(me + 4 * shift, count), side)
    met = peers + depth + has_prev.astype(jnp.int32) + has_next.astype(jnp.int32)

    def loop(low, high, step):
        def body(index, carry):
            step(index)
            return carry

        lax.fori_loop(low, high, body, 0)

    def remote(src, dst, send, recv, context, tensor=side):
        return pltpu.make_async_remote_copy(
            src_ref=src, dst_ref=dst, send_sem=send, recv_sem=recv,
            device_id=(context, tensor), device_id_type=MESH,
        )

    def halo_copy(group):
        return remote(
            halo_out.at[group], halo_in.at[group], halo_ss.at[group], halo_rs.at[group],
            lax.rem(me + 1, count),
        )

    def x_copy(group):
        return remote(x_out.at[group], x_in.at[group], x_ss.at[group], x_rs.at[group], x_peer)

    def y_copy(group):
        return remote(y_out.at[group], y_in.at[group], y_ss.at[group], y_rs.at[group], y_peer)

    def z_copy(group, shift):
        return remote(
            z_out.at[group], z_in.at[group, shift - 1],
            z_ss.at[group, shift - 1], z_rs.at[group, shift - 1],
            lax.rem(me + 4 * shift, count),
        )

    def to_wire(value):
        return value.reshape(order * sub, 128).astype(BF16) if wire == BF16 else value

    def from_wire(value):
        return value.astype(F32).reshape(order, sub, 128) if wire == BF16 else value

    for i in range(3):
        param_copy(i).wait()

    def spread(l):
        lanes = pl.ds(pl.multiple_of(l * 128, 128), 128)
        for i in range(3):
            base = pl.multiple_of((i * tiles + l) * 8, 8)
            taps_raw[pl.ds(base, tap_count), :] = filter_ref[i, :, lanes]
        for part in range(order // 8):
            base = pl.multiple_of((part * tiles + l) * 8, 8)
            modes[0, pl.ds(base, 8), :] = decay_ref[part * 8 : part * 8 + 8, lanes]
            modes[1, pl.ds(base, 8), :] = residue_ref[part * 8 : part * 8 + 8, lanes]

    loop(0, tiles, spread)

    def prepare(group):
        for i in range(3):
            for j in range(tap_count):
                start = i * pitch + group * span + j
                taps[group, i, j] = taps_raw[pl.ds(start, sub, stride=8), :]
        for m in range(order):
            start = ((m // 8) * tiles + group * sub) * 8 + m % 8
            rate = modes[0, pl.ds(start, sub, stride=8), :]
            residue = modes[1, pl.ds(start, sub, stride=8), :]
            pole[group, 0, m] = jnp.exp(-rate)
            pole[group, 1, m] = jnp.exp(-rate * float(row_count))
            pole[group, 2, m] = jnp.exp(-rate * float(row_count - 8))
            pole[group, 3, m] = jnp.exp(-rate * 8.0)
            weight[group, m] = residue * jnp.sqrt(1.0 - jnp.exp(-2.0 * rate))

    loop(0, groups, prepare)
    for i in range(3):
        edge_copy(i).wait()

    def pack(group):
        for i in range(3):
            for l in range(sub):
                lanes = pl.ds(pl.multiple_of((group * sub + l) * 128, 128), 128)
                last = edge[i, :, lanes].astype(F32)
                mix[(i * sub + l) * 8 : (i * sub + l + 1) * 8, :] = last[8:16]
        halo_out[group] = mix[0 : 3 * span, :].astype(BF16)

    loop(0, groups, pack)
    pl.semaphore_wait(barrier, met)

    @pl.when(has_next)
    def _():
        loop(0, groups, lambda group: halo_copy(group).start())

    def convolve(i, group, block):
        f = [taps[group, i, j] for j in range(tap_count)]
        rows = [rows_x[i, group, block * 8 + 8 + r] for r in range(1 - tap_count, 8)]
        outs = []
        for r in range(8):
            acc = rows[r + tap_count - 1] * f[0]
            for j in range(1, tap_count):
                acc = acc + rows[r + tap_count - 1 - j] * f[j]
            outs.append(acc)
        return outs

    def convert(chosen, group):
        for i in chosen:
            input_copy(i, group).wait()

        def body(pair, carry):
            at = pl.ds(pl.multiple_of(pair * 16, 16), 16)
            for i in chosen:
                for l in range(sub):
                    tile = group * sub + l
                    lanes = pl.ds(pl.multiple_of(tile * 128, 128), 128)
                    value = inputs[i, at, lanes].astype(F32)
                    for half in range(2):
                        start = half * span + l * 8
                        turn[i, start : start + 8, :] = value[half * 8 : half * 8 + 8]
            for i in chosen:
                for r in range(16):
                    start = (r // 8) * span + r % 8
                    rows_x[i, group, pair * 16 + 8 + r] = turn[i, pl.ds(start, sub, stride=8), :]
            return carry

        lax.fori_loop(0, blocks // 2, body, 0)

    def place_halo(chosen, group):
        @pl.when(has_prev)
        def _():
            for i in chosen:
                turn[i, 0:span, :] = halo_in[group, i * span : (i + 1) * span, :].astype(F32)
            for i in chosen:
                for r in range(8):
                    rows_x[i, group, r] = turn[i, pl.ds(r, sub, stride=8), :]

        @pl.when(jnp.logical_not(has_prev))
        def _():
            for i in chosen:
                rows_x[i, group, 0:8] = jnp.zeros((8, sub, 128), F32)

    def scan_block(group, block, h):
        keys = convolve(1, group, block)
        values = convolve(2, group, block)
        a = pole[group, 0]
        for r in range(8):
            p = keys[r] * values[r]
            prod[block * 8 + r, group] = p
            h = a * h + p[None]
        return h

    zero_state = jnp.zeros((order, sub, 128), F32)

    def phase_a(group):
        convert((1, 2), group)

        def body(block, h):
            starts[group, block] = h
            return scan_block(group, block, h)

        h = lax.fori_loop(1, blocks, body, zero_state)
        state[group] = h
        pl.when(has_prev)(lambda: halo_copy(group).wait_recv())
        place_halo((1, 2), group)
        first = scan_block(group, 0, zero_state)
        first_ref[group] = first
        e = state[group] + pole[group, 2] * first
        state[group] = e
        x_out[group] = to_wire(e)
        x_copy(group).start()

    def stage_y(group):
        x_copy(group).wait_recv()
        other = from_wire(x_in[group])
        own = state[group]
        b = pole[group, 1]
        both = jnp.where(x == 1, b * other + own, b * own + other)
        prefix[group] = other * x.astype(F32)
        plane[group] = both
        y_out[group] = to_wire(both)
        y_copy(group).start()

    def stage_z(group):
        y_copy(group).wait_recv()
        other = from_wire(y_in[group])
        own = plane[group]
        b = pole[group, 1]
        b2 = b * b
        all4 = jnp.where(y == 1, b2 * other + own, b2 * own + other)
        here = prefix[group]
        prefix[group] = jnp.where(y == 1, here + jnp.where(x == 1, b, 1.0) * other, here)
        z_out[group] = to_wire(all4)
        for shift in range(1, depth):
            pl.when(z + shift < depth)(lambda shift=shift: z_copy(group, shift).start())

    def stage_end(group):
        b = pole[group, 1]
        b2 = b * b
        b4 = b2 * b2
        column[...] = zero_state
        for shift in range(depth - 1, 0, -1):

            @pl.when(z >= shift)
            def _(shift=shift):
                z_copy(group, shift).wait_recv()
                column[...] = b4 * column[...] + from_wire(z_in[group, shift - 1])

        scale = jnp.where(x == 1, b, 1.0) * jnp.where(y == 1, b2, 1.0)
        prefix[group] = prefix[group] + scale * column[...]

    def phase_b(group):
        convert((0,), group)
        place_halo((0,), group)

        def body(block, carry):
            gates = convolve(0, group, block)
            for r in range(8):
                gate[block * 8 + r, group] = gates[r]
            return carry

        lax.fori_loop(0, blocks, body, 0)
        a = pole[group, 0]
        w = weight[group]
        direct[group, 0] = jnp.sum(w, axis=0) + skip_ref[group]
        for r in range(8):
            w = w * a
            table[group, r] = w
            if r < 7:
                direct[group, r + 1] = jnp.sum(w, axis=0)

    def phase_c(group):
        def emit(block, s):
            p = [prod[block * 8 + r, group] for r in range(8)]
            for r in range(8):
                value = jnp.sum(table[group, r] * s, axis=0)
                near = direct[group, 0] * p[r]
                for j in range(1, r + 1):
                    near = near + direct[group, j] * p[r - j]
                start = block * pitch + group * span + r
                mix[pl.ds(start, sub, stride=8), :] = gate[block * 8 + r, group] * (value + near)

        a8 = pole[group, 3]
        s = prefix[group]
        emit(0, s)

        def body(block, s):
            emit(block, s + starts[group, block])
            return pole[group, 3] * s

        lax.fori_loop(1, blocks, body, a8 * s + first_ref[group])

    def forward(group):
        phase_a(group)
        pl.when(group >= 1)(lambda: stage_y(group - 1))
        pl.when(group >= 2)(lambda: stage_z(group - 2))

    def backward(group):
        stage_end(group)
        phase_c(group)

    loop(0, groups, forward)
    param_copy(3).wait()
    loop(0, groups // 2, phase_b)
    stage_y(groups - 1)
    if groups >= 2:
        stage_z(groups - 2)
    loop(groups // 2, groups, phase_b)
    stage_z(groups - 1)
    loop(0, groups, backward)
    param_copy(4).wait()

    def out_copy(pair):
        at = pl.ds(pl.multiple_of(pair * 16, 16), 16)
        return pltpu.make_async_copy(mixed.at[at], mixed_hbm.at[at], out_sem.at[pair])

    def finish(pair, carry):
        at = pl.ds(pl.multiple_of(pair * 16, 16), 16)
        squares = jnp.zeros((16, 128), F32)
        for l in range(tiles):
            parts = []
            for half in range(2):
                start = pl.multiple_of((pair * 2 + half) * pitch + l * 8, 8)
                parts.append(mix[pl.ds(start, 8), :])
            rounded = jnp.concatenate(parts, axis=0).astype(BF16)
            lanes = slice(l * 128, l * 128 + 128)
            mixed[at, lanes] = rounded
            summed = residual_ref[at, lanes].astype(F32) + rounded.astype(F32)
            squares = squares + summed * summed
        sq_out[at, :] = squares
        out_copy(pair).start()
        return carry

    lax.fori_loop(0, blocks // 2, finish, 0)

    def sq_copy(shift):
        return remote(
            sq_out, sq_in.at[shift - 1], sq_ss.at[shift - 1], sq_rs.at[shift - 1],
            me, lax.rem(side + shift, peers),
        )

    for shift in range(1, peers):
        sq_copy(shift).start()
    for shift in range(1, peers):
        sq_copy(shift).wait_recv()

    squares = sq_out[...]
    for shift in range(1, peers):
        squares = squares + sq_in[shift - 1]
    squares_ref[...] = squares

    def drain(pair, carry):
        out_copy(pair).wait()
        return carry

    lax.fori_loop(0, blocks // 2, drain, 0)
    for shift in range(1, peers):
        sq_copy(shift).wait_send()

    def settle(group):
        x_copy(group).wait_send()
        y_copy(group).wait_send()
        for shift in range(1, depth):
            pl.when(z + shift < depth)(lambda shift=shift: z_copy(group, shift).wait_send())
        pl.when(has_next)(lambda: halo_copy(group).wait_send())

    loop(0, groups, settle)


def normalise(
    width, mixed_hbm, residual_hbm, squares_ref, gain_ref, out_hbm, normed_hbm,
    mixed, residual, normed, scale_ref, mixed_sem, residual_sem, out_sem, normed_sem,
):
    row_count, channels = mixed_hbm.shape
    tall = 16
    pieces = row_count // tall

    ends = (
        (mixed_hbm, mixed, mixed_sem), (residual_hbm, residual, residual_sem),
        (mixed, out_hbm, out_sem), (normed, normed_hbm, normed_sem),
    )

    def copy(kind, piece):
        source, target, sems = ends[kind]
        at = pl.ds(pl.multiple_of(piece * tall, tall), tall)
        return pltpu.make_async_copy(source.at[at], target.at[at], sems.at[piece])

    def loop(step):
        def body(index, carry):
            step(index)
            return carry

        lax.fori_loop(0, pieces, body, 0)

    def fetch(piece):
        copy(0, piece).start()
        copy(1, piece).start()

    loop(fetch)
    mean = jnp.sum(squares_ref[...], axis=1, keepdims=True) / float(width)
    scale_ref[...] = jnp.broadcast_to(lax.rsqrt(mean + 1e-05), (row_count, 128))

    def work(piece):
        copy(0, piece).wait()
        copy(2, piece).start()
        copy(1, piece).wait()
        at = pl.ds(pl.multiple_of(piece * tall, tall), tall)
        scale = scale_ref[at, :]
        for l in range(channels // 128):
            lanes = slice(l * 128, l * 128 + 128)
            summed = residual[at, lanes].astype(F32) + mixed[at, lanes].astype(F32)
            normed[at, lanes] = (summed * scale * gain_ref[:, lanes]).astype(BF16)
        copy(3, piece).start()

    loop(work)

    def drain(piece):
        copy(2, piece).wait()
        copy(3, piece).wait()

    loop(drain)


def shards(
    count, peers,
    query_proj, key_proj, value_proj, short_filter, residues, decay, skip_gain, residual, norm_gain
):
    rows, channels = query_proj.shape
    order = decay.shape[0]
    tap_count = short_filter.shape[1]
    tiles = channels // 128
    sub = min(8, tiles)
    groups = tiles // sub
    depth = count // 4
    wire = BF16 if sub == 8 else F32
    packet = (order * sub, 128) if wire == BF16 else (order, sub, 128)
    others = max(1, peers - 1)
    packets = pltpu.VMEM((groups, *packet), wire)
    modal = pltpu.VMEM((groups, order, sub, 128), F32)
    by_row = pltpu.VMEM((rows, groups, sub, 128), F32)
    dma = pltpu.SemaphoreType.DMA
    hbm = pl.BlockSpec(memory_space=pltpu.HBM)
    whole = pl.BlockSpec(memory_space=pltpu.VMEM)
    out = jax.ShapeDtypeStruct((rows, channels), BF16)
    mixed, squares = pl.pallas_call(
        functools.partial(kernel, count, peers, wire),
        out_shape=(out, jax.ShapeDtypeStruct((rows, 128), F32)),
        in_specs=[hbm] * 8,
        out_specs=(hbm, whole),
        scratch_shapes=[
            pltpu.VMEM((3, rows, channels), BF16),
            pltpu.VMEM((3, tap_count, channels), F32),
            pltpu.VMEM((order, channels), F32),
            pltpu.VMEM((order, channels), F32),
            pltpu.VMEM((groups, sub, 128), F32),
            pltpu.VMEM((rows, channels), BF16),
            pltpu.VMEM((3, 16, channels), BF16),
            pltpu.VMEM((3, groups, rows + 8, sub, 128), F32),
            pltpu.VMEM((3, 16 * sub, 128), F32),
            pltpu.VMEM((groups, 3, tap_count, sub, 128), F32),
            pltpu.VMEM((3 * tiles * 8, 128), F32),
            pltpu.VMEM((2, order * tiles, 128), F32),
            pltpu.VMEM((groups, 4, order, sub, 128), F32),
            modal,
            pltpu.VMEM((groups, 8, order, sub, 128), F32),
            pltpu.VMEM((groups, 8, sub, 128), F32),
            by_row, by_row,
            pltpu.VMEM((groups, rows // 8, order, sub, 128), F32),
            pltpu.VMEM((rows * tiles, 128), F32),
            pltpu.VMEM((rows, channels), BF16),
            modal, modal, modal, modal,
            pltpu.VMEM((order, sub, 128), F32),
            pltpu.VMEM((groups, 3 * sub * 8, 128), BF16),
            pltpu.VMEM((groups, 3 * sub * 8, 128), BF16),
            packets, packets, packets, packets, packets,
            pltpu.VMEM((groups, depth - 1, *packet), wire),
            pltpu.VMEM((rows, 128), F32), pltpu.VMEM((others, rows, 128), F32),
            dma((3, groups)), dma((5,)), dma((3,)), dma((rows // 16,)),
            dma((groups,)), dma((groups,)), dma((groups,)), dma((groups,)),
            dma((groups,)), dma((groups,)), dma((groups, depth - 1)), dma((groups, depth - 1)),
            dma((others,)), dma((others,)),
        ],
        compiler_params=pltpu.CompilerParams(
            collective_id=0, has_side_effects=True, vmem_limit_bytes=60 * 1024 * 1024
        ),
    )(
        query_proj, key_proj, value_proj, short_filter, residues, decay,
        skip_gain.reshape(groups, sub, 128), residual,
    )
    pieces = rows // 16
    block = pltpu.VMEM((rows, channels), BF16)
    return pl.pallas_call(
        functools.partial(normalise, channels * peers),
        out_shape=(out, out),
        in_specs=[hbm, hbm, whole, whole],
        out_specs=(hbm, hbm),
        scratch_shapes=[
            block, block, block, pltpu.VMEM((rows, 128), F32), dma((pieces,)), dma((pieces,)), dma((pieces,)), dma((pieces,))
        ],
        compiler_params=pltpu.CompilerParams(vmem_limit_bytes=60 * 1024 * 1024),
    )(mixed, residual, squares, norm_gain.reshape(1, channels))


def solution(mesh):
    in_specs = (
        P("context", "tensor"),
        P("context", "tensor"),
        P("context", "tensor"),
        P(None, None, "tensor"),
        P(None, "tensor"),
        P(None, "tensor"),
        P("tensor"),
        P("context", "tensor"),
        P("tensor"),
    )
    out_specs = (P("context", "tensor"), P("context", "tensor"))
    return jax.shard_map(
        functools.partial(shards, mesh.shape["context"], mesh.shape["tensor"]),
        mesh=mesh, in_specs=in_specs, out_specs=out_specs, check_vma=False,
    )
```

```python
import functools

import jax
import jax.numpy as jnp
from jax import lax
from jax.experimental import pallas as pl
from jax.experimental.pallas import tpu as pltpu
from jax.sharding import PartitionSpec as P

MESH = pl.DeviceIdType.MESH
F32 = jnp.float32
BF16 = jnp.bfloat16


def kernel(
    count, peers, wire,
    q_hbm, k_hbm, v_hbm, filter_hbm, residue_hbm, decay_hbm, skip_hbm, residual_hbm,
    mixed_hbm, squares_ref,
    inputs, filter_ref, residue_ref, decay_ref, skip_ref, residual_ref, edge,
    rows_x, turn, taps, taps_raw, modes, pole, weight, table, direct, prod, gate, starts, mix, mixed,
    state, first_ref, prefix, plane, column,
    halo_out, halo_in, x_out, x_in, y_out, y_in, z_out, z_in, sq_out, sq_in,
    in_sem, par_sem, edge_sem, out_sem,
    halo_ss, halo_rs, x_ss, x_rs, y_ss, y_rs, z_ss, z_rs, sq_ss, sq_rs,
):
    row_count, channels = q_hbm.shape
    tap_count = filter_hbm.shape[1]
    order = decay_hbm.shape[0]
    tiles = channels // 128
    sub = min(8, tiles)
    groups = tiles // sub
    blocks = row_count // 8
    pitch = tiles * 8
    span = sub * 8
    me = lax.axis_index("context")
    side = lax.axis_index("tensor")
    x = lax.rem(me, 2)
    y = lax.rem(me // 2, 2)
    z = me // 4
    depth = count // 4
    x_peer = me + 1 - 2 * x
    y_peer = me + 2 - 4 * y
    has_prev, has_next = me > 0, me < count - 1

    sources = (q_hbm, k_hbm, v_hbm)

    def edge_copy(i):
        return pltpu.make_async_copy(
            sources[i].at[row_count - 16 : row_count], edge.at[i], edge_sem.at[i]
        )

    def input_copy(i, group):
        lanes = pl.ds(pl.multiple_of(group * sub * 128, 128), sub * 128)
        return pltpu.make_async_copy(
            sources[i].at[:, lanes], inputs.at[i, :, lanes], in_sem.at[i, group]
        )

    params = (
        (decay_hbm, decay_ref), (residue_hbm, residue_ref), (filter_hbm, filter_ref),
        (skip_hbm, skip_ref), (residual_hbm, residual_ref),
    )

    def param_copy(i):
        return pltpu.make_async_copy(params[i][0], params[i][1], par_sem.at[i])

    for i in range(3):
        edge_copy(i).start()
    for i in range(3):
        param_copy(i).start()
    for group in range(groups):
        input_copy(1, group).start()
        input_copy(2, group).start()
    for group in range(groups):
        input_copy(0, group).start()
    for i in range(3, 5):
        param_copy(i).start()

    barrier = pltpu.get_barrier_semaphore()

    def greet(context, tensor):
        pl.semaphore_signal(barrier, inc=1, device_id=(context, tensor), device_id_type=MESH)

    greet(x_peer, side)
    greet(y_peer, side)
    for shift in range(1, peers):
        greet(me, lax.rem(side + shift, peers))
    pl.when(has_prev)(lambda: greet(me - 1, side))
    pl.when(has_next)(lambda: greet(me + 1, side))
    for shift in range(1, depth):
        greet(lax.rem(me + 4 * shift, count), side)
    met = peers + depth + has_prev.astype(jnp.int32) + has_next.astype(jnp.int32)

    def loop(low, high, step):
        def body(index, carry):
            step(index)
            return carry

        lax.fori_loop(low, high, body, 0)

    def remote(src, dst, send, recv, context, tensor=side):
        return pltpu.make_async_remote_copy(
            src_ref=src, dst_ref=dst, send_sem=send, recv_sem=recv,
            device_id=(context, tensor), device_id_type=MESH,
        )

    def halo_copy(group, part):
        at = pl.ds(span, 2 * span) if part == 0 else pl.ds(0, span)
        return remote(
            halo_out.at[group, at], halo_in.at[group, at],
            halo_ss.at[group, part], halo_rs.at[group, part], lax.rem(me + 1, count),
        )

    def x_copy(group):
        return remote(x_out.at[group], x_in.at[group], x_ss.at[group], x_rs.at[group], x_peer)

    def y_copy(group):
        return remote(y_out.at[group], y_in.at[group], y_ss.at[group], y_rs.at[group], y_peer)

    def z_copy(group, shift):
        return remote(
            z_out.at[group], z_in.at[group, shift - 1],
            z_ss.at[group, shift - 1], z_rs.at[group, shift - 1],
            lax.rem(me + 4 * shift, count),
        )

    def to_wire(value):
        return value.reshape(order * sub, 128).astype(BF16) if wire == BF16 else value

    def from_wire(value):
        return value.astype(F32).reshape(order, sub, 128) if wire == BF16 else value

    for i in range(3):
        param_copy(i).wait()

    def spread(l):
        lanes = pl.ds(pl.multiple_of(l * 128, 128), 128)
        for i in range(3):
            base = pl.multiple_of((i * tiles + l) * 8, 8)
            taps_raw[pl.ds(base, tap_count), :] = filter_ref[i, :, lanes]
        for part in range(order // 8):
            base = pl.multiple_of((part * tiles + l) * 8, 8)
            modes[0, pl.ds(base, 8), :] = decay_ref[part * 8 : part * 8 + 8, lanes]
            modes[1, pl.ds(base, 8), :] = residue_ref[part * 8 : part * 8 + 8, lanes]

    loop(0, tiles, spread)

    def prepare(group):
        for i in range(3):
            for j in range(tap_count):
                start = i * pitch + group * span + j
                taps[group, i, j] = taps_raw[pl.ds(start, sub, stride=8), :]
        for m in range(order):
            start = ((m // 8) * tiles + group * sub) * 8 + m % 8
            rate = modes[0, pl.ds(start, sub, stride=8), :]
            residue = modes[1, pl.ds(start, sub, stride=8), :]
            pole[group, 0, m] = jnp.exp(-rate)
            pole[group, 1, m] = jnp.exp(-rate * float(row_count))
            pole[group, 2, m] = jnp.exp(-rate * float(row_count - 8))
            pole[group, 3, m] = jnp.exp(-rate * 8.0)
            weight[group, m] = residue * jnp.sqrt(1.0 - jnp.exp(-2.0 * rate))

    loop(0, groups, prepare)
    for i in range(3):
        edge_copy(i).wait()

    def pack(group):
        for i in range(3):
            for l in range(sub):
                lanes = pl.ds(pl.multiple_of((group * sub + l) * 128, 128), 128)
                last = edge[i, :, lanes].astype(F32)
                mix[(i * sub + l) * 8 : (i * sub + l + 1) * 8, :] = last[8:16]
        halo_out[group] = mix[0 : 3 * span, :].astype(BF16)

    loop(0, groups, pack)
    pl.semaphore_wait(barrier, met)

    @pl.when(has_next)
    def _():
        halo_copy(0, 0).start()

    def convolve(i, group, block):
        f = [taps[group, i, j] for j in range(tap_count)]
        rows = [rows_x[i, group, block * 8 + 8 + r] for r in range(1 - tap_count, 8)]
        outs = []
        for r in range(8):
            acc = rows[r + tap_count - 1] * f[0]
            for j in range(1, tap_count):
                acc = acc + rows[r + tap_count - 1 - j] * f[j]
            outs.append(acc)
        return outs

    def convert(chosen, group):
        for i in chosen:
            input_copy(i, group).wait()

        def body(pair, carry):
            at = pl.ds(pl.multiple_of(pair * 16, 16), 16)
            for i in chosen:
                for l in range(sub):
                    tile = group * sub + l
                    lanes = pl.ds(pl.multiple_of(tile * 128, 128), 128)
                    value = inputs[i, at, lanes].astype(F32)
                    for half in range(2):
                        start = half * span + l * 8
                        turn[i, start : start + 8, :] = value[half * 8 : half * 8 + 8]
            for i in chosen:
                for r in range(16):
                    start = (r // 8) * span + r % 8
                    rows_x[i, group, pair * 16 + 8 + r] = turn[i, pl.ds(start, sub, stride=8), :]
            return carry

        lax.fori_loop(0, blocks // 2, body, 0)

    def place_halo(chosen, group):
        @pl.when(has_prev)
        def _():
            for i in chosen:
                turn[i, 0:span, :] = halo_in[group, i * span : (i + 1) * span, :].astype(F32)
            for i in chosen:
                for r in range(8):
                    rows_x[i, group, r] = turn[i, pl.ds(r, sub, stride=8), :]

        @pl.when(jnp.logical_not(has_prev))
        def _():
            for i in chosen:
                rows_x[i, group, 0:8] = jnp.zeros((8, sub, 128), F32)

    def scan_block(group, block, h):
        keys = convolve(1, group, block)
        values = convolve(2, group, block)
        a = pole[group, 0]
        for r in range(8):
            p = keys[r] * values[r]
            prod[block * 8 + r, group] = p
            h = a * h + p[None]
        return h

    zero_state = jnp.zeros((order, sub, 128), F32)

    def phase_a(group):
        @pl.when(jnp.logical_and(has_next, group + 1 < groups))
        def _():
            halo_copy(group + 1, 0).start()

        convert((1, 2), group)

        def body(block, h):
            starts[group, block] = h
            return scan_block(group, block, h)

        h = lax.fori_loop(1, blocks, body, zero_state)
        state[group] = h
        pl.when(has_prev)(lambda: halo_copy(group, 0).wait_recv())
        place_halo((1, 2), group)
        first = scan_block(group, 0, zero_state)
        first_ref[group] = first
        e = state[group] + pole[group, 2] * first
        state[group] = e
        x_out[group] = to_wire(e)
        x_copy(group).start()
        pl.when(has_next)(lambda: halo_copy(group, 1).start())

    def stage_y(group):
        x_copy(group).wait_recv()
        other = from_wire(x_in[group])
        own = state[group]
        b = pole[group, 1]
        both = jnp.where(x == 1, b * other + own, b * own + other)
        prefix[group] = other * x.astype(F32)
        plane[group] = both
        y_out[group] = to_wire(both)
        y_copy(group).start()

    def stage_z(group):
        y_copy(group).wait_recv()
        other = from_wire(y_in[group])
        own = plane[group]
        b = pole[group, 1]
        b2 = b * b
        all4 = jnp.where(y == 1, b2 * other + own, b2 * own + other)
        here = prefix[group]
        prefix[group] = jnp.where(y == 1, here + jnp.where(x == 1, b, 1.0) * other, here)
        z_out[group] = to_wire(all4)
        for shift in range(1, depth):
            pl.when(z + shift < depth)(lambda shift=shift: z_copy(group, shift).start())

    def stage_end(group):
        b = pole[group, 1]
        b2 = b * b
        b4 = b2 * b2
        column[...] = zero_state
        for shift in range(depth - 1, 0, -1):

            @pl.when(z >= shift)
            def _(shift=shift):
                z_copy(group, shift).wait_recv()
                column[...] = b4 * column[...] + from_wire(z_in[group, shift - 1])

        scale = jnp.where(x == 1, b, 1.0) * jnp.where(y == 1, b2, 1.0)
        prefix[group] = prefix[group] + scale * column[...]

    def phase_b(group):
        convert((0,), group)
        pl.when(has_prev)(lambda: halo_copy(group, 1).wait_recv())
        place_halo((0,), group)

        def body(block, carry):
            gates = convolve(0, group, block)
            for r in range(8):
                gate[block * 8 + r, group] = gates[r]
            return carry

        lax.fori_loop(0, blocks, body, 0)
        a = pole[group, 0]
        w = weight[group]
        direct[group, 0] = jnp.sum(w, axis=0) + skip_ref[group]
        for r in range(8):
            w = w * a
            table[group, r] = w
            if r < 7:
                direct[group, r + 1] = jnp.sum(w, axis=0)

    def phase_c(group):
        def emit(block, s):
            p = [prod[block * 8 + r, group] for r in range(8)]
            for r in range(8):
                value = jnp.sum(table[group, r] * s, axis=0)
                near = direct[group, 0] * p[r]
                for j in range(1, r + 1):
                    near = near + direct[group, j] * p[r - j]
                start = block * pitch + group * span + r
                mix[pl.ds(start, sub, stride=8), :] = gate[block * 8 + r, group] * (value + near)

        a8 = pole[group, 3]
        s = prefix[group]
        emit(0, s)

        def body(block, s):
            emit(block, s + starts[group, block])
            return pole[group, 3] * s

        lax.fori_loop(1, blocks, body, a8 * s + first_ref[group])

    def forward(group):
        phase_a(group)
        pl.when(group >= 1)(lambda: stage_y(group - 1))
        pl.when(group >= 2)(lambda: stage_z(group - 2))

    def backward(group):
        stage_end(group)
        phase_c(group)

    loop(0, groups, forward)
    param_copy(3).wait()
    loop(0, groups // 2, phase_b)
    stage_y(groups - 1)
    if groups >= 2:
        stage_z(groups - 2)
    loop(groups // 2, groups, phase_b)
    stage_z(groups - 1)
    loop(0, groups, backward)
    param_copy(4).wait()

    def out_copy(pair):
        at = pl.ds(pl.multiple_of(pair * 16, 16), 16)
        return pltpu.make_async_copy(mixed.at[at], mixed_hbm.at[at], out_sem.at[pair])

    def finish(pair, carry):
        at = pl.ds(pl.multiple_of(pair * 16, 16), 16)
        squares = jnp.zeros((16, 128), F32)
        for l in range(tiles):
            parts = []
            for half in range(2):
                start = pl.multiple_of((pair * 2 + half) * pitch + l * 8, 8)
                parts.append(mix[pl.ds(start, 8), :])
            rounded = jnp.concatenate(parts, axis=0).astype(BF16)
            lanes = slice(l * 128, l * 128 + 128)
            mixed[at, lanes] = rounded
            summed = residual_ref[at, lanes].astype(F32) + rounded.astype(F32)
            squares = squares + summed * summed
        sq_out[at, :] = squares
        out_copy(pair).start()
        return carry

    lax.fori_loop(0, blocks // 2, finish, 0)

    def sq_copy(shift):
        return remote(
            sq_out, sq_in.at[shift - 1], sq_ss.at[shift - 1], sq_rs.at[shift - 1],
            me, lax.rem(side + shift, peers),
        )

    for shift in range(1, peers):
        sq_copy(shift).start()
    for shift in range(1, peers):
        sq_copy(shift).wait_recv()

    squares = sq_out[...]
    for shift in range(1, peers):
        squares = squares + sq_in[shift - 1]
    squares_ref[...] = squares

    def drain(pair, carry):
        out_copy(pair).wait()
        return carry

    lax.fori_loop(0, blocks // 2, drain, 0)
    for shift in range(1, peers):
        sq_copy(shift).wait_send()

    def settle(group):
        x_copy(group).wait_send()
        y_copy(group).wait_send()
        for shift in range(1, depth):
            pl.when(z + shift < depth)(lambda shift=shift: z_copy(group, shift).wait_send())

        @pl.when(has_next)
        def _():
            halo_copy(group, 0).wait_send()
            halo_copy(group, 1).wait_send()

    loop(0, groups, settle)


def normalise(
    width, mixed_hbm, residual_hbm, squares_hbm, gain_hbm, out_hbm, normed_hbm,
    mixed, residual, normed, squares_ref, gain_ref, scale_ref, small_sem, mixed_sem, residual_sem, out_sem, normed_sem,
):
    row_count, channels = mixed_hbm.shape
    tall = 16
    pieces = row_count // tall

    ends = (
        (mixed_hbm, mixed, mixed_sem), (residual_hbm, residual, residual_sem),
        (mixed, out_hbm, out_sem), (normed, normed_hbm, normed_sem),
    )

    def copy(kind, piece):
        source, target, sems = ends[kind]
        at = pl.ds(pl.multiple_of(piece * tall, tall), tall)
        return pltpu.make_async_copy(source.at[at], target.at[at], sems.at[piece])

    def loop(step):
        def body(index, carry):
            step(index)
            return carry

        lax.fori_loop(0, pieces, body, 0)

    def fetch(piece):
        copy(0, piece).start()
        copy(1, piece).start()

    small = (
        pltpu.make_async_copy(squares_hbm, squares_ref, small_sem.at[0]),
        pltpu.make_async_copy(gain_hbm, gain_ref, small_sem.at[1]),
    )
    small[0].start()
    small[1].start()
    loop(fetch)
    small[0].wait()
    small[1].wait()
    mean = jnp.sum(squares_ref[...], axis=1, keepdims=True) / float(width)
    scale_ref[...] = jnp.broadcast_to(lax.rsqrt(mean + 1e-05), (row_count, 128))

    def work(piece):
        copy(0, piece).wait()
        copy(2, piece).start()
        copy(1, piece).wait()
        at = pl.ds(pl.multiple_of(piece * tall, tall), tall)
        scale = scale_ref[at, :]
        for l in range(channels // 128):
            lanes = slice(l * 128, l * 128 + 128)
            summed = residual[at, lanes].astype(F32) + mixed[at, lanes].astype(F32)
            normed[at, lanes] = (summed * scale * gain_ref[:, lanes]).astype(BF16)
        copy(3, piece).start()

    loop(work)

    def drain(piece):
        copy(2, piece).wait()
        copy(3, piece).wait()

    loop(drain)


def shards(
    count, peers,
    query_proj, key_proj, value_proj, short_filter, residues, decay, skip_gain, residual, norm_gain
):
    rows, channels = query_proj.shape
    order = decay.shape[0]
    tap_count = short_filter.shape[1]
    tiles = channels // 128
    sub = min(8, tiles)
    groups = tiles // sub
    depth = count // 4
    wire = BF16 if sub == 8 else F32
    packet = (order * sub, 128) if wire == BF16 else (order, sub, 128)
    others = max(1, peers - 1)
    packets = pltpu.VMEM((groups, *packet), wire)
    modal = pltpu.VMEM((groups, order, sub, 128), F32)
    by_row = pltpu.VMEM((rows, groups, sub, 128), F32)
    dma = pltpu.SemaphoreType.DMA
    hbm = pl.BlockSpec(memory_space=pltpu.HBM)
    whole = pl.BlockSpec(memory_space=pltpu.VMEM)
    out = jax.ShapeDtypeStruct((rows, channels), BF16)
    mixed, squares = pl.pallas_call(
        functools.partial(kernel, count, peers, wire),
        out_shape=(out, jax.ShapeDtypeStruct((rows, 128), F32)),
        in_specs=[hbm] * 8,
        out_specs=(hbm, whole),
        scratch_shapes=[
            pltpu.VMEM((3, rows, channels), BF16),
            pltpu.VMEM((3, tap_count, channels), F32),
            pltpu.VMEM((order, channels), F32),
            pltpu.VMEM((order, channels), F32),
            pltpu.VMEM((groups, sub, 128), F32),
            pltpu.VMEM((rows, channels), BF16),
            pltpu.VMEM((3, 16, channels), BF16),
            pltpu.VMEM((3, groups, rows + 8, sub, 128), F32),
            pltpu.VMEM((3, 16 * sub, 128), F32),
            pltpu.VMEM((groups, 3, tap_count, sub, 128), F32),
            pltpu.VMEM((3 * tiles * 8, 128), F32),
            pltpu.VMEM((2, order * tiles, 128), F32),
            pltpu.VMEM((groups, 4, order, sub, 128), F32),
            modal,
            pltpu.VMEM((groups, 8, order, sub, 128), F32),
            pltpu.VMEM((groups, 8, sub, 128), F32),
            by_row, by_row,
            pltpu.VMEM((groups, rows // 8, order, sub, 128), F32),
            pltpu.VMEM((rows * tiles, 128), F32),
            pltpu.VMEM((rows, channels), BF16),
            modal, modal, modal, modal,
            pltpu.VMEM((order, sub, 128), F32),
            pltpu.VMEM((groups, 3 * sub * 8, 128), BF16),
            pltpu.VMEM((groups, 3 * sub * 8, 128), BF16),
            packets, packets, packets, packets, packets,
            pltpu.VMEM((groups, depth - 1, *packet), wire),
            pltpu.VMEM((rows, 128), F32), pltpu.VMEM((others, rows, 128), F32),
            dma((3, groups)), dma((5,)), dma((3,)), dma((rows // 16,)),
            dma((groups, 2)), dma((groups, 2)), dma((groups,)), dma((groups,)),
            dma((groups,)), dma((groups,)), dma((groups, depth - 1)), dma((groups, depth - 1)),
            dma((others,)), dma((others,)),
        ],
        compiler_params=pltpu.CompilerParams(
            collective_id=0, has_side_effects=True, vmem_limit_bytes=60 * 1024 * 1024
        ),
    )(
        query_proj, key_proj, value_proj, short_filter, residues, decay,
        skip_gain.reshape(groups, sub, 128), residual,
    )
    pieces = rows // 16
    block = pltpu.VMEM((rows, channels), BF16)
    return pl.pallas_call(
        functools.partial(normalise, channels * peers),
        out_shape=(out, out),
        in_specs=[hbm] * 4,
        out_specs=(hbm, hbm),
        scratch_shapes=[
            block, block, block, pltpu.VMEM((rows, 128), F32), pltpu.VMEM((1, channels), F32),
            pltpu.VMEM((rows, 128), F32), dma((2,)), dma((pieces,)), dma((pieces,)), dma((pieces,)), dma((pieces,))
        ],
        compiler_params=pltpu.CompilerParams(vmem_limit_bytes=60 * 1024 * 1024),
    )(mixed, residual, squares, norm_gain.reshape(1, channels))


def solution(mesh):
    in_specs = (
        P("context", "tensor"),
        P("context", "tensor"),
        P("context", "tensor"),
        P(None, None, "tensor"),
        P(None, "tensor"),
        P(None, "tensor"),
        P("tensor"),
        P("context", "tensor"),
        P("tensor"),
    )
    out_specs = (P("context", "tensor"), P("context", "tensor"))
    return jax.shard_map(
        functools.partial(shards, mesh.shape["context"], mesh.shape["tensor"]),
        mesh=mesh, in_specs=in_specs, out_specs=out_specs, check_vma=False,
    )
```

```python
import functools

import jax
import jax.numpy as jnp
from jax import lax
from jax.experimental import pallas as pl
from jax.experimental.pallas import tpu as pltpu
from jax.sharding import PartitionSpec as P

MESH = pl.DeviceIdType.MESH
F32 = jnp.float32
BF16 = jnp.bfloat16


def kernel(
    count, peers, wire,
    q_hbm, k_hbm, v_hbm, filter_hbm, residue_hbm, decay_hbm, skip_hbm, residual_hbm,
    mixed_hbm, squares_ref,
    inputs, filter_ref, residue_ref, decay_ref, skip_ref, residual_ref, edge,
    rows_x, turn, taps, taps_raw, modes, pole, weight, table, direct, prod, gate, starts, mix, mixed,
    state, first_ref, prefix, plane,
    halo_out, halo_in, x_out, x_in, y_out, y_in, z_out, z_in, sq_out, sq_in,
    in_sem, par_sem, edge_sem, out_sem,
    halo_ss, halo_rs, x_ss, x_rs, y_ss, y_rs, z_ss, z_rs, sq_ss, sq_rs,
):
    row_count, channels = q_hbm.shape
    tap_count = filter_hbm.shape[1]
    order = decay_hbm.shape[0]
    tiles = channels // 128
    sub = min(8, tiles)
    groups = tiles // sub
    blocks = row_count // 8
    pitch = tiles * 8
    span = sub * 8
    me = lax.axis_index("context")
    side = lax.axis_index("tensor")
    x = lax.rem(me, 2)
    y = lax.rem(me // 2, 2)
    z = me // 4
    depth = count // 4
    x_peer = me + 1 - 2 * x
    y_peer = me + 2 - 4 * y
    has_prev, has_next = me > 0, me < count - 1
    has_down, has_up = z > 0, z < depth - 1

    sources = (q_hbm, k_hbm, v_hbm)

    def edge_copy(i):
        return pltpu.make_async_copy(
            sources[i].at[row_count - 16 : row_count], edge.at[i], edge_sem.at[i]
        )

    def input_copy(i, group):
        lanes = pl.ds(pl.multiple_of(group * sub * 128, 128), sub * 128)
        return pltpu.make_async_copy(
            sources[i].at[:, lanes], inputs.at[i, :, lanes], in_sem.at[i, group]
        )

    params = (
        (decay_hbm, decay_ref), (residue_hbm, residue_ref), (filter_hbm, filter_ref),
        (skip_hbm, skip_ref), (residual_hbm, residual_ref),
    )

    def param_copy(i):
        return pltpu.make_async_copy(params[i][0], params[i][1], par_sem.at[i])

    for i in range(3):
        edge_copy(i).start()
    for i in range(3):
        param_copy(i).start()
    for group in range(groups):
        input_copy(1, group).start()
        input_copy(2, group).start()
    for group in range(groups):
        input_copy(0, group).start()
    for i in range(3, 5):
        param_copy(i).start()

    barrier = pltpu.get_barrier_semaphore()

    def greet(context, tensor):
        pl.semaphore_signal(barrier, inc=1, device_id=(context, tensor), device_id_type=MESH)

    greet(x_peer, side)
    greet(y_peer, side)
    for shift in range(1, peers):
        greet(me, lax.rem(side + shift, peers))
    pl.when(has_prev)(lambda: greet(me - 1, side))
    pl.when(has_next)(lambda: greet(me + 1, side))
    pl.when(has_down)(lambda: greet(me - 4, side))
    pl.when(has_up)(lambda: greet(me + 4, side))
    met = (
        1 + peers + has_prev.astype(jnp.int32) + has_next.astype(jnp.int32)
        + has_down.astype(jnp.int32) + has_up.astype(jnp.int32)
    )

    def loop(low, high, step):
        def body(index, carry):
            step(index)
            return carry

        lax.fori_loop(low, high, body, 0)

    def remote(src, dst, send, recv, context, tensor=side):
        return pltpu.make_async_remote_copy(
            src_ref=src, dst_ref=dst, send_sem=send, recv_sem=recv,
            device_id=(context, tensor), device_id_type=MESH,
        )

    def halo_copy(group, part):
        at = pl.ds(span, 2 * span) if part == 0 else pl.ds(0, span)
        return remote(
            halo_out.at[group, at], halo_in.at[group, at],
            halo_ss.at[group, part], halo_rs.at[group, part], lax.rem(me + 1, count),
        )

    def x_copy(group):
        return remote(x_out.at[group], x_in.at[group], x_ss.at[group], x_rs.at[group], x_peer)

    def y_copy(group):
        return remote(y_out.at[group], y_in.at[group], y_ss.at[group], y_rs.at[group], y_peer)

    def z_copy(group):
        return remote(
            z_out.at[group], z_in.at[group], z_ss.at[group], z_rs.at[group],
            lax.rem(me + 4, count),
        )

    def to_wire(value):
        return value.reshape(order * sub, 128).astype(BF16) if wire == BF16 else value

    def from_wire(value):
        return value.astype(F32).reshape(order, sub, 128) if wire == BF16 else value

    for i in range(3):
        param_copy(i).wait()

    def spread(l):
        lanes = pl.ds(pl.multiple_of(l * 128, 128), 128)
        for i in range(3):
            base = pl.multiple_of((i * tiles + l) * 8, 8)
            taps_raw[pl.ds(base, tap_count), :] = filter_ref[i, :, lanes]
        for part in range(order // 8):
            base = pl.multiple_of((part * tiles + l) * 8, 8)
            modes[0, pl.ds(base, 8), :] = decay_ref[part * 8 : part * 8 + 8, lanes]
            modes[1, pl.ds(base, 8), :] = residue_ref[part * 8 : part * 8 + 8, lanes]

    loop(0, tiles, spread)

    def prepare(group):
        for i in range(3):
            for j in range(tap_count):
                start = i * pitch + group * span + j
                taps[group, i, j] = taps_raw[pl.ds(start, sub, stride=8), :]
        for m in range(order):
            start = ((m // 8) * tiles + group * sub) * 8 + m % 8
            rate = modes[0, pl.ds(start, sub, stride=8), :]
            residue = modes[1, pl.ds(start, sub, stride=8), :]
            pole[group, 0, m] = jnp.exp(-rate)
            pole[group, 1, m] = jnp.exp(-rate * float(row_count))
            pole[group, 2, m] = jnp.exp(-rate * float(row_count - 8))
            pole[group, 3, m] = jnp.exp(-rate * 8.0)
            weight[group, m] = residue * jnp.sqrt(1.0 - jnp.exp(-2.0 * rate))

    loop(0, groups, prepare)
    for i in range(3):
        edge_copy(i).wait()

    def pack(group):
        for i in range(3):
            for l in range(sub):
                lanes = pl.ds(pl.multiple_of((group * sub + l) * 128, 128), 128)
                last = edge[i, :, lanes].astype(F32)
                mix[(i * sub + l) * 8 : (i * sub + l + 1) * 8, :] = last[8:16]
        halo_out[group] = mix[0 : 3 * span, :].astype(BF16)

    loop(0, groups, pack)
    pl.semaphore_wait(barrier, met)

    @pl.when(has_next)
    def _():
        halo_copy(0, 0).start()

    def convolve(i, group, block):
        f = [taps[group, i, j] for j in range(tap_count)]
        rows = [rows_x[i, group, block * 8 + 8 + r] for r in range(1 - tap_count, 8)]
        outs = []
        for r in range(8):
            acc = rows[r + tap_count - 1] * f[0]
            for j in range(1, tap_count):
                acc = acc + rows[r + tap_count - 1 - j] * f[j]
            outs.append(acc)
        return outs

    def convert(chosen, group):
        for i in chosen:
            input_copy(i, group).wait()

        def body(pair, carry):
            at = pl.ds(pl.multiple_of(pair * 16, 16), 16)
            for i in chosen:
                for l in range(sub):
                    tile = group * sub + l
                    lanes = pl.ds(pl.multiple_of(tile * 128, 128), 128)
                    value = inputs[i, at, lanes].astype(F32)
                    for half in range(2):
                        start = half * span + l * 8
                        turn[i, start : start + 8, :] = value[half * 8 : half * 8 + 8]
            for i in chosen:
                for r in range(16):
                    start = (r // 8) * span + r % 8
                    rows_x[i, group, pair * 16 + 8 + r] = turn[i, pl.ds(start, sub, stride=8), :]
            return carry

        lax.fori_loop(0, blocks // 2, body, 0)

    def place_halo(chosen, group):
        @pl.when(has_prev)
        def _():
            for i in chosen:
                turn[i, 0:span, :] = halo_in[group, i * span : (i + 1) * span, :].astype(F32)
            for i in chosen:
                for r in range(8):
                    rows_x[i, group, r] = turn[i, pl.ds(r, sub, stride=8), :]

        @pl.when(jnp.logical_not(has_prev))
        def _():
            for i in chosen:
                rows_x[i, group, 0:8] = jnp.zeros((8, sub, 128), F32)

    def scan_block(group, block, h):
        keys = convolve(1, group, block)
        values = convolve(2, group, block)
        a = pole[group, 0]
        for r in range(8):
            p = keys[r] * values[r]
            prod[block * 8 + r, group] = p
            h = a * h + p[None]
        return h

    zero_state = jnp.zeros((order, sub, 128), F32)

    def phase_a(group):
        @pl.when(jnp.logical_and(has_next, group + 1 < groups))
        def _():
            halo_copy(group + 1, 0).start()

        convert((1, 2), group)

        def body(block, h):
            starts[group, block] = h
            return scan_block(group, block, h)

        h = lax.fori_loop(1, blocks, body, zero_state)
        state[group] = h
        pl.when(has_prev)(lambda: halo_copy(group, 0).wait_recv())
        place_halo((1, 2), group)
        first = scan_block(group, 0, zero_state)
        first_ref[group] = first
        e = state[group] + pole[group, 2] * first
        state[group] = e
        x_out[group] = to_wire(e)
        x_copy(group).start()
        pl.when(has_next)(lambda: halo_copy(group, 1).start())

    def stage_y(group):
        x_copy(group).wait_recv()
        other = from_wire(x_in[group])
        own = state[group]
        b = pole[group, 1]
        both = jnp.where(x == 1, b * other + own, b * own + other)
        prefix[group] = other * x.astype(F32)
        plane[group] = both
        y_out[group] = to_wire(both)
        y_copy(group).start()

    def stage_z(group):
        y_copy(group).wait_recv()
        other = from_wire(y_in[group])
        own = plane[group]
        b = pole[group, 1]
        b2 = b * b
        all4 = jnp.where(y == 1, b2 * other + own, b2 * own + other)
        here = prefix[group]
        prefix[group] = jnp.where(y == 1, here + jnp.where(x == 1, b, 1.0) * other, here)
        plane[group] = all4

        @pl.when(jnp.logical_and(z == 0, has_up))
        def _():
            z_out[group] = to_wire(all4)
            z_copy(group).start()

    def stage_end(group):
        z_copy(group).wait_recv()
        other = from_wire(z_in[group])
        b = pole[group, 1]
        b2 = b * b

        @pl.when(has_up)
        def _():
            z_out[group] = to_wire(b2 * b2 * other + plane[group])
            z_copy(group).start()

        scale = jnp.where(x == 1, b, 1.0) * jnp.where(y == 1, b2, 1.0)
        prefix[group] = prefix[group] + scale * other

    def phase_b(group):
        convert((0,), group)
        pl.when(has_prev)(lambda: halo_copy(group, 1).wait_recv())
        place_halo((0,), group)

        def body(block, carry):
            gates = convolve(0, group, block)
            for r in range(8):
                gate[block * 8 + r, group] = gates[r]
            return carry

        lax.fori_loop(0, blocks, body, 0)
        a = pole[group, 0]
        w = weight[group]
        direct[group, 0] = jnp.sum(w, axis=0) + skip_ref[group]
        for r in range(8):
            w = w * a
            table[group, r] = w
            if r < 7:
                direct[group, r + 1] = jnp.sum(w, axis=0)

    def phase_c(group):
        def emit(block, s):
            p = [prod[block * 8 + r, group] for r in range(8)]
            for r in range(8):
                value = jnp.sum(table[group, r] * s, axis=0)
                near = direct[group, 0] * p[r]
                for j in range(1, r + 1):
                    near = near + direct[group, j] * p[r - j]
                start = block * pitch + group * span + r
                mix[pl.ds(start, sub, stride=8), :] = gate[block * 8 + r, group] * (value + near)

        a8 = pole[group, 3]
        s = prefix[group]
        emit(0, s)

        def body(block, s):
            emit(block, s + starts[group, block])
            return pole[group, 3] * s

        lax.fori_loop(1, blocks, body, a8 * s + first_ref[group])

    def forward(group):
        phase_a(group)
        pl.when(group >= 1)(lambda: stage_y(group - 1))
        pl.when(group >= 2)(lambda: stage_z(group - 2))

    def end_at(turn_of, group):
        @pl.when(z == turn_of if turn_of < 3 else z >= 3)
        def _():
            stage_end(group)

    loop(0, groups, forward)
    param_copy(3).wait()
    if groups == 4:
        end_at(1, 0)
        loop(0, 2, phase_b)
        stage_y(3)
        stage_z(2)
        end_at(1, 1)
        end_at(2, 0)
        loop(2, 4, phase_b)
        stage_z(3)

        def backward(group):
            end_at(3, group)
            pl.when(group < 3)(lambda: end_at(2, group + 1))
            pl.when(group < 2)(lambda: end_at(1, group + 2))
            phase_c(group)

        loop(0, 4, backward)
    else:
        loop(0, groups, phase_b)
        stage_y(groups - 1)
        if groups >= 2:
            stage_z(groups - 2)
        stage_z(groups - 1)

        def backward(group):
            pl.when(has_down)(lambda: stage_end(group))
            phase_c(group)

        loop(0, groups, backward)

    param_copy(4).wait()

    def out_copy(pair):
        at = pl.ds(pl.multiple_of(pair * 16, 16), 16)
        return pltpu.make_async_copy(mixed.at[at], mixed_hbm.at[at], out_sem.at[pair])

    def finish(pair, carry):
        at = pl.ds(pl.multiple_of(pair * 16, 16), 16)
        squares = jnp.zeros((16, 128), F32)
        for l in range(tiles):
            parts = []
            for half in range(2):
                start = pl.multiple_of((pair * 2 + half) * pitch + l * 8, 8)
                parts.append(mix[pl.ds(start, 8), :])
            rounded = jnp.concatenate(parts, axis=0).astype(BF16)
            lanes = slice(l * 128, l * 128 + 128)
            mixed[at, lanes] = rounded
            summed = residual_ref[at, lanes].astype(F32) + rounded.astype(F32)
            squares = squares + summed * summed
        sq_out[at, :] = squares
        out_copy(pair).start()
        return carry

    lax.fori_loop(0, blocks // 2, finish, 0)

    def sq_copy(shift):
        return remote(
            sq_out, sq_in.at[shift - 1], sq_ss.at[shift - 1], sq_rs.at[shift - 1],
            me, lax.rem(side + shift, peers),
        )

    for shift in range(1, peers):
        sq_copy(shift).start()
    for shift in range(1, peers):
        sq_copy(shift).wait_recv()

    squares = sq_out[...]
    for shift in range(1, peers):
        squares = squares + sq_in[shift - 1]
    squares_ref[...] = squares

    def drain(pair, carry):
        out_copy(pair).wait()
        return carry

    lax.fori_loop(0, blocks // 2, drain, 0)
    for shift in range(1, peers):
        sq_copy(shift).wait_send()

    def settle(group):
        x_copy(group).wait_send()
        y_copy(group).wait_send()
        pl.when(has_up)(lambda: z_copy(group).wait_send())

        @pl.when(has_next)
        def _():
            halo_copy(group, 0).wait_send()
            halo_copy(group, 1).wait_send()

    loop(0, groups, settle)


def normalise(
    width, mixed_hbm, residual_hbm, squares_hbm, gain_hbm, out_hbm, normed_hbm,
    mixed, residual, normed, squares_ref, gain_ref, scale_ref, small_sem, mixed_sem, residual_sem, out_sem, normed_sem,
):
    row_count, channels = mixed_hbm.shape
    tall = 16
    pieces = row_count // tall

    ends = (
        (mixed_hbm, mixed, mixed_sem), (residual_hbm, residual, residual_sem),
        (mixed, out_hbm, out_sem), (normed, normed_hbm, normed_sem),
    )

    def copy(kind, piece):
        source, target, sems = ends[kind]
        at = pl.ds(pl.multiple_of(piece * tall, tall), tall)
        return pltpu.make_async_copy(source.at[at], target.at[at], sems.at[piece])

    def loop(step):
        def body(index, carry):
            step(index)
            return carry

        lax.fori_loop(0, pieces, body, 0)

    def fetch(piece):
        copy(0, piece).start()
        copy(1, piece).start()

    small = (
        pltpu.make_async_copy(squares_hbm, squares_ref, small_sem.at[0]),
        pltpu.make_async_copy(gain_hbm, gain_ref, small_sem.at[1]),
    )
    small[0].start()
    small[1].start()
    loop(fetch)
    small[0].wait()
    small[1].wait()
    mean = jnp.sum(squares_ref[...], axis=1, keepdims=True) / float(width)
    scale_ref[...] = jnp.broadcast_to(lax.rsqrt(mean + 1e-05), (row_count, 128))

    def work(piece):
        copy(0, piece).wait()
        copy(2, piece).start()
        copy(1, piece).wait()
        at = pl.ds(pl.multiple_of(piece * tall, tall), tall)
        scale = scale_ref[at, :]
        for l in range(channels // 128):
            lanes = slice(l * 128, l * 128 + 128)
            summed = residual[at, lanes].astype(F32) + mixed[at, lanes].astype(F32)
            normed[at, lanes] = (summed * scale * gain_ref[:, lanes]).astype(BF16)
        copy(3, piece).start()

    loop(work)

    def drain(piece):
        copy(2, piece).wait()
        copy(3, piece).wait()

    loop(drain)


def shards(
    count, peers,
    query_proj, key_proj, value_proj, short_filter, residues, decay, skip_gain, residual, norm_gain
):
    rows, channels = query_proj.shape
    order = decay.shape[0]
    tap_count = short_filter.shape[1]
    tiles = channels // 128
    sub = min(8, tiles)
    groups = tiles // sub
    wire = BF16 if sub == 8 else F32
    packet = (order * sub, 128) if wire == BF16 else (order, sub, 128)
    others = max(1, peers - 1)
    packets = pltpu.VMEM((groups, *packet), wire)
    modal = pltpu.VMEM((groups, order, sub, 128), F32)
    by_row = pltpu.VMEM((rows, groups, sub, 128), F32)
    dma = pltpu.SemaphoreType.DMA
    hbm = pl.BlockSpec(memory_space=pltpu.HBM)
    whole = pl.BlockSpec(memory_space=pltpu.VMEM)
    out = jax.ShapeDtypeStruct((rows, channels), BF16)
    mixed, squares = pl.pallas_call(
        functools.partial(kernel, count, peers, wire),
        out_shape=(out, jax.ShapeDtypeStruct((rows, 128), F32)),
        in_specs=[hbm] * 8,
        out_specs=(hbm, whole),
        scratch_shapes=[
            pltpu.VMEM((3, rows, channels), BF16),
            pltpu.VMEM((3, tap_count, channels), F32),
            pltpu.VMEM((order, channels), F32),
            pltpu.VMEM((order, channels), F32),
            pltpu.VMEM((groups, sub, 128), F32),
            pltpu.VMEM((rows, channels), BF16),
            pltpu.VMEM((3, 16, channels), BF16),
            pltpu.VMEM((3, groups, rows + 8, sub, 128), F32),
            pltpu.VMEM((3, 16 * sub, 128), F32),
            pltpu.VMEM((groups, 3, tap_count, sub, 128), F32),
            pltpu.VMEM((3 * tiles * 8, 128), F32),
            pltpu.VMEM((2, order * tiles, 128), F32),
            pltpu.VMEM((groups, 4, order, sub, 128), F32),
            modal,
            pltpu.VMEM((groups, 8, order, sub, 128), F32),
            pltpu.VMEM((groups, 8, sub, 128), F32),
            by_row, by_row,
            pltpu.VMEM((groups, rows // 8, order, sub, 128), F32),
            pltpu.VMEM((rows * tiles, 128), F32),
            pltpu.VMEM((rows, channels), BF16),
            modal, modal, modal, modal,
            pltpu.VMEM((groups, 3 * sub * 8, 128), BF16),
            pltpu.VMEM((groups, 3 * sub * 8, 128), BF16),
            packets, packets, packets, packets, packets, packets,
            pltpu.VMEM((rows, 128), F32), pltpu.VMEM((others, rows, 128), F32),
            dma((3, groups)), dma((5,)), dma((3,)), dma((rows // 16,)),
            dma((groups, 2)), dma((groups, 2)), dma((groups,)), dma((groups,)),
            dma((groups,)), dma((groups,)), dma((groups,)), dma((groups,)),
            dma((others,)), dma((others,)),
        ],
        compiler_params=pltpu.CompilerParams(
            collective_id=0, has_side_effects=True, vmem_limit_bytes=60 * 1024 * 1024
        ),
    )(
        query_proj, key_proj, value_proj, short_filter, residues, decay,
        skip_gain.reshape(groups, sub, 128), residual,
    )
    pieces = rows // 16
    block = pltpu.VMEM((rows, channels), BF16)
    return pl.pallas_call(
        functools.partial(normalise, channels * peers),
        out_shape=(out, out),
        in_specs=[hbm] * 4,
        out_specs=(hbm, hbm),
        scratch_shapes=[
            block, block, block, pltpu.VMEM((rows, 128), F32), pltpu.VMEM((1, channels), F32),
            pltpu.VMEM((rows, 128), F32), dma((2,)), dma((pieces,)), dma((pieces,)), dma((pieces,)), dma((pieces,))
        ],
        compiler_params=pltpu.CompilerParams(vmem_limit_bytes=60 * 1024 * 1024),
    )(mixed, residual, squares, norm_gain.reshape(1, channels))


def solution(mesh):
    in_specs = (
        P("context", "tensor"),
        P("context", "tensor"),
        P("context", "tensor"),
        P(None, None, "tensor"),
        P(None, "tensor"),
        P(None, "tensor"),
        P("tensor"),
        P("context", "tensor"),
        P("tensor"),
    )
    out_specs = (P("context", "tensor"), P("context", "tensor"))
    return jax.shard_map(
        functools.partial(shards, mesh.shape["context"], mesh.shape["tensor"]),
        mesh=mesh, in_specs=in_specs, out_specs=out_specs, check_vma=False,
    )
```

```python
import functools

import jax
import jax.numpy as jnp
from jax import lax
from jax.experimental import pallas as pl
from jax.experimental.pallas import tpu as pltpu
from jax.sharding import PartitionSpec as P

MESH = pl.DeviceIdType.MESH
F32 = jnp.float32
BF16 = jnp.bfloat16


def kernel(
    count, peers, wire,
    q_hbm, k_hbm, v_hbm, filter_hbm, residue_hbm, decay_hbm, skip_hbm, residual_hbm,
    mixed_hbm, squares_ref,
    inputs, filter_ref, residue_ref, decay_ref, skip_ref, residual_ref, edge,
    rows_x, turn, taps, taps_raw, modes, pole, weight, table, direct, prod, gate, starts, mix, mixed,
    state, first_ref, prefix, plane, column,
    halo_out, halo_in, x_out, x_in, y_out, y_in, z_out, z_in, sq_out, sq_in,
    in_sem, par_sem, edge_sem, out_sem,
    halo_ss, halo_rs, x_ss, x_rs, y_ss, y_rs, z_ss, z_rs, sq_ss, sq_rs,
):
    row_count, channels = q_hbm.shape
    tap_count = filter_hbm.shape[1]
    order = decay_hbm.shape[0]
    tiles = channels // 128
    sub = min(8, tiles)
    groups = tiles // sub
    blocks = row_count // 8
    several = 3 if (blocks - 1) % 3 == 0 else 1
    pitch = tiles * 8
    span = sub * 8
    me = lax.axis_index("context")
    side = lax.axis_index("tensor")
    x = lax.rem(me, 2)
    y = lax.rem(me // 2, 2)
    z = me // 4
    depth = count // 4
    x_peer = me + 1 - 2 * x
    y_peer = me + 2 - 4 * y
    has_prev, has_next = me > 0, me < count - 1

    sources = (q_hbm, k_hbm, v_hbm)

    def edge_copy(i):
        return pltpu.make_async_copy(
            sources[i].at[row_count - 16 : row_count], edge.at[i], edge_sem.at[i]
        )

    def input_copy(i, group):
        lanes = pl.ds(pl.multiple_of(group * sub * 128, 128), sub * 128)
        return pltpu.make_async_copy(
            sources[i].at[:, lanes], inputs.at[i, :, lanes], in_sem.at[i, group]
        )

    params = (
        (decay_hbm, decay_ref), (residue_hbm, residue_ref), (filter_hbm, filter_ref),
        (skip_hbm, skip_ref), (residual_hbm, residual_ref),
    )

    def param_copy(i):
        return pltpu.make_async_copy(params[i][0], params[i][1], par_sem.at[i])

    for i in range(3):
        edge_copy(i).start()
    for i in range(3):
        param_copy(i).start()
    for group in range(groups):
        input_copy(1, group).start()
        input_copy(2, group).start()
    for group in range(groups):
        input_copy(0, group).start()
    for i in range(3, 5):
        param_copy(i).start()

    barrier = pltpu.get_barrier_semaphore()

    def greet(context, tensor):
        pl.semaphore_signal(barrier, inc=1, device_id=(context, tensor), device_id_type=MESH)

    greet(x_peer, side)
    greet(y_peer, side)
    for shift in range(1, peers):
        greet(me, lax.rem(side + shift, peers))
    pl.when(has_prev)(lambda: greet(me - 1, side))
    pl.when(has_next)(lambda: greet(me + 1, side))
    for shift in range(1, depth):
        greet(lax.rem(me + 4 * shift, count), side)
    met = peers + depth + has_prev.astype(jnp.int32) + has_next.astype(jnp.int32)

    def loop(low, high, step):
        def body(index, carry):
            step(index)
            return carry

        lax.fori_loop(low, high, body, 0)

    def remote(src, dst, send, recv, context, tensor=side):
        return pltpu.make_async_remote_copy(
            src_ref=src, dst_ref=dst, send_sem=send, recv_sem=recv,
            device_id=(context, tensor), device_id_type=MESH,
        )

    def halo_copy(group, part):
        at = pl.ds(span, 2 * span) if part == 0 else pl.ds(0, span)
        return remote(
            halo_out.at[group, at], halo_in.at[group, at],
            halo_ss.at[group, part], halo_rs.at[group, part], lax.rem(me + 1, count),
        )

    def x_copy(group):
        return remote(x_out.at[group], x_in.at[group], x_ss.at[group], x_rs.at[group], x_peer)

    def y_copy(group):
        return remote(y_out.at[group], y_in.at[group], y_ss.at[group], y_rs.at[group], y_peer)

    def z_copy(group, shift):
        return remote(
            z_out.at[group], z_in.at[group, shift - 1],
            z_ss.at[group, shift - 1], z_rs.at[group, shift - 1],
            lax.rem(me + 4 * shift, count),
        )

    def to_wire(value):
        return value.reshape(order * sub, 128).astype(BF16) if wire == BF16 else value

    def from_wire(value):
        return value.astype(F32).reshape(order, sub, 128) if wire == BF16 else value

    for i in range(3):
        param_copy(i).wait()

    def spread(l):
        lanes = pl.ds(pl.multiple_of(l * 128, 128), 128)
        for i in range(3):
            base = pl.multiple_of((i * tiles + l) * 8, 8)
            taps_raw[pl.ds(base, tap_count), :] = filter_ref[i, :, lanes]
        for part in range(order // 8):
            base = pl.multiple_of((part * tiles + l) * 8, 8)
            modes[0, pl.ds(base, 8), :] = decay_ref[part * 8 : part * 8 + 8, lanes]
            modes[1, pl.ds(base, 8), :] = residue_ref[part * 8 : part * 8 + 8, lanes]

    loop(0, tiles, spread)

    def prepare(group):
        for i in range(3):
            for j in range(tap_count):
                start = i * pitch + group * span + j
                taps[group, i, j] = taps_raw[pl.ds(start, sub, stride=8), :]
        for m in range(order):
            start = ((m // 8) * tiles + group * sub) * 8 + m % 8
            rate = modes[0, pl.ds(start, sub, stride=8), :]
            residue = modes[1, pl.ds(start, sub, stride=8), :]
            pole[group, 0, m] = jnp.exp(-rate)
            pole[group, 1, m] = jnp.exp(-rate * float(row_count))
            pole[group, 2, m] = jnp.exp(-rate * float(row_count - 8))
            pole[group, 3, m] = jnp.exp(-rate * 8.0)
            weight[group, m] = residue * jnp.sqrt(1.0 - jnp.exp(-2.0 * rate))

    loop(0, groups, prepare)
    for i in range(3):
        edge_copy(i).wait()

    def pack(group):
        for i in range(3):
            for l in range(sub):
                lanes = pl.ds(pl.multiple_of((group * sub + l) * 128, 128), 128)
                last = edge[i, :, lanes].astype(F32)
                mix[(i * sub + l) * 8 : (i * sub + l + 1) * 8, :] = last[8:16]
        halo_out[group] = mix[0 : 3 * span, :].astype(BF16)

    loop(0, groups, pack)
    pl.semaphore_wait(barrier, met)

    @pl.when(has_next)
    def _():
        halo_copy(0, 0).start()

    def convolve(i, group, block):
        f = [taps[group, i, j] for j in range(tap_count)]
        rows = [rows_x[i, group, block * 8 + 8 + r] for r in range(1 - tap_count, 8)]
        outs = []
        for r in range(8):
            acc = rows[r + tap_count - 1] * f[0]
            for j in range(1, tap_count):
                acc = acc + rows[r + tap_count - 1 - j] * f[j]
            outs.append(acc)
        return outs

    def convert(chosen, group):
        for i in chosen:
            input_copy(i, group).wait()

        def body(pair, carry):
            at = pl.ds(pl.multiple_of(pair * 16, 16), 16)
            for i in chosen:
                for l in range(sub):
                    tile = group * sub + l
                    lanes = pl.ds(pl.multiple_of(tile * 128, 128), 128)
                    value = inputs[i, at, lanes].astype(F32)
                    for half in range(2):
                        start = half * span + l * 8
                        turn[i, start : start + 8, :] = value[half * 8 : half * 8 + 8]
            for i in chosen:
                for r in range(16):
                    start = (r // 8) * span + r % 8
                    rows_x[i, group, pair * 16 + 8 + r] = turn[i, pl.ds(start, sub, stride=8), :]
            return carry

        lax.fori_loop(0, blocks // 2, body, 0)

    def place_halo(chosen, group):
        @pl.when(has_prev)
        def _():
            for i in chosen:
                turn[i, 0:span, :] = halo_in[group, i * span : (i + 1) * span, :].astype(F32)
            for i in chosen:
                for r in range(8):
                    rows_x[i, group, r] = turn[i, pl.ds(r, sub, stride=8), :]

        @pl.when(jnp.logical_not(has_prev))
        def _():
            for i in chosen:
                rows_x[i, group, 0:8] = jnp.zeros((8, sub, 128), F32)

    def scan_block(group, block, h):
        keys = convolve(1, group, block)
        values = convolve(2, group, block)
        a = pole[group, 0]
        for r in range(8):
            p = keys[r] * values[r]
            prod[block * 8 + r, group] = p
            h = a * h + p[None]
        return h

    zero_state = jnp.zeros((order, sub, 128), F32)

    def phase_a(group):
        @pl.when(jnp.logical_and(has_next, group + 1 < groups))
        def _():
            halo_copy(group + 1, 0).start()

        convert((1, 2), group)

        def body(step, h):
            for k in range(several):
                block = 1 + step * several + k
                starts[group, block] = h
                h = scan_block(group, block, h)
            return h

        h = lax.fori_loop(0, (blocks - 1) // several, body, zero_state)
        state[group] = h
        pl.when(has_prev)(lambda: halo_copy(group, 0).wait_recv())
        place_halo((1, 2), group)
        first = scan_block(group, 0, zero_state)
        first_ref[group] = first
        e = state[group] + pole[group, 2] * first
        state[group] = e
        x_out[group] = to_wire(e)
        x_copy(group).start()
        pl.when(has_next)(lambda: halo_copy(group, 1).start())

    def stage_y(group):
        x_copy(group).wait_recv()
        other = from_wire(x_in[group])
        own = state[group]
        b = pole[group, 1]
        both = jnp.where(x == 1, b * other + own, b * own + other)
        prefix[group] = other * x.astype(F32)
        plane[group] = both
        y_out[group] = to_wire(both)
        y_copy(group).start()

    def stage_z(group):
        y_copy(group).wait_recv()
        other = from_wire(y_in[group])
        own = plane[group]
        b = pole[group, 1]
        b2 = b * b
        all4 = jnp.where(y == 1, b2 * other + own, b2 * own + other)
        here = prefix[group]
        prefix[group] = jnp.where(y == 1, here + jnp.where(x == 1, b, 1.0) * other, here)
        z_out[group] = to_wire(all4)
        for shift in range(1, depth):
            pl.when(z + shift < depth)(lambda shift=shift: z_copy(group, shift).start())

    def stage_end(group):
        b = pole[group, 1]
        b2 = b * b
        b4 = b2 * b2
        column[...] = zero_state
        for shift in range(depth - 1, 0, -1):

            @pl.when(z >= shift)
            def _(shift=shift):
                z_copy(group, shift).wait_recv()
                column[...] = b4 * column[...] + from_wire(z_in[group, shift - 1])

        scale = jnp.where(x == 1, b, 1.0) * jnp.where(y == 1, b2, 1.0)
        prefix[group] = prefix[group] + scale * column[...]

    def phase_b(group):
        convert((0,), group)
        pl.when(has_prev)(lambda: halo_copy(group, 1).wait_recv())
        place_halo((0,), group)

        def body(pair, carry):
            for k in range(2):
                block = pair * 2 + k
                gates = convolve(0, group, block)
                for r in range(8):
                    gate[block * 8 + r, group] = gates[r]
            return carry

        lax.fori_loop(0, blocks // 2, body, 0)
        a = pole[group, 0]
        w = weight[group]
        direct[group, 0] = jnp.sum(w, axis=0) + skip_ref[group]
        for r in range(8):
            w = w * a
            table[group, r] = w
            if r < 7:
                direct[group, r + 1] = jnp.sum(w, axis=0)

    def phase_c(group):
        def emit(block, s):
            p = [prod[block * 8 + r, group] for r in range(8)]
            for r in range(8):
                value = jnp.sum(table[group, r] * s, axis=0)
                near = direct[group, 0] * p[r]
                for j in range(1, r + 1):
                    near = near + direct[group, j] * p[r - j]
                start = block * pitch + group * span + r
                mix[pl.ds(start, sub, stride=8), :] = gate[block * 8 + r, group] * (value + near)

        a8 = pole[group, 3]
        s = prefix[group]
        emit(0, s)

        def body(step, s):
            for k in range(several):
                block = 1 + step * several + k
                emit(block, s + starts[group, block])
                s = pole[group, 3] * s
            return s

        lax.fori_loop(0, (blocks - 1) // several, body, a8 * s + first_ref[group])

    def forward(group):
        phase_a(group)
        pl.when(group >= 1)(lambda: stage_y(group - 1))
        pl.when(group >= 2)(lambda: stage_z(group - 2))

    def backward(group):
        stage_end(group)
        phase_c(group)

    loop(0, groups, forward)
    param_copy(3).wait()
    loop(0, groups // 2, phase_b)
    stage_y(groups - 1)
    if groups >= 2:
        stage_z(groups - 2)
    loop(groups // 2, groups, phase_b)
    stage_z(groups - 1)
    loop(0, groups, backward)
    param_copy(4).wait()

    def out_copy(pair):
        at = pl.ds(pl.multiple_of(pair * 16, 16), 16)
        return pltpu.make_async_copy(mixed.at[at], mixed_hbm.at[at], out_sem.at[pair])

    def finish(pair, carry):
        at = pl.ds(pl.multiple_of(pair * 16, 16), 16)
        squares = jnp.zeros((16, 128), F32)
        for l in range(tiles):
            parts = []
            for half in range(2):
                start = pl.multiple_of((pair * 2 + half) * pitch + l * 8, 8)
                parts.append(mix[pl.ds(start, 8), :])
            rounded = jnp.concatenate(parts, axis=0).astype(BF16)
            lanes = slice(l * 128, l * 128 + 128)
            mixed[at, lanes] = rounded
            summed = residual_ref[at, lanes].astype(F32) + rounded.astype(F32)
            squares = squares + summed * summed
        sq_out[at, :] = squares
        out_copy(pair).start()
        return carry

    lax.fori_loop(0, blocks // 2, finish, 0)

    def sq_copy(shift):
        return remote(
            sq_out, sq_in.at[shift - 1], sq_ss.at[shift - 1], sq_rs.at[shift - 1],
            me, lax.rem(side + shift, peers),
        )

    for shift in range(1, peers):
        sq_copy(shift).start()
    for shift in range(1, peers):
        sq_copy(shift).wait_recv()

    squares = sq_out[...]
    for shift in range(1, peers):
        squares = squares + sq_in[shift - 1]
    squares_ref[...] = squares

    def drain(pair, carry):
        out_copy(pair).wait()
        return carry

    lax.fori_loop(0, blocks // 2, drain, 0)
    for shift in range(1, peers):
        sq_copy(shift).wait_send()

    def settle(group):
        x_copy(group).wait_send()
        y_copy(group).wait_send()
        for shift in range(1, depth):
            pl.when(z + shift < depth)(lambda shift=shift: z_copy(group, shift).wait_send())

        @pl.when(has_next)
        def _():
            halo_copy(group, 0).wait_send()
            halo_copy(group, 1).wait_send()

    loop(0, groups, settle)


def normalise(
    width, mixed_hbm, residual_hbm, squares_hbm, gain_hbm, out_hbm, normed_hbm,
    mixed, residual, normed, squares_ref, gain_ref, scale_ref, small_sem, mixed_sem, residual_sem, out_sem, normed_sem,
):
    row_count, channels = mixed_hbm.shape
    tall = 16
    pieces = row_count // tall

    ends = (
        (mixed_hbm, mixed, mixed_sem), (residual_hbm, residual, residual_sem),
        (mixed, out_hbm, out_sem), (normed, normed_hbm, normed_sem),
    )

    def copy(kind, piece):
        source, target, sems = ends[kind]
        at = pl.ds(pl.multiple_of(piece * tall, tall), tall)
        return pltpu.make_async_copy(source.at[at], target.at[at], sems.at[piece])

    def loop(step):
        def body(index, carry):
            step(index)
            return carry

        lax.fori_loop(0, pieces, body, 0)

    def fetch(piece):
        copy(0, piece).start()
        copy(1, piece).start()

    small = (
        pltpu.make_async_copy(squares_hbm, squares_ref, small_sem.at[0]),
        pltpu.make_async_copy(gain_hbm, gain_ref, small_sem.at[1]),
    )
    small[0].start()
    small[1].start()
    loop(fetch)
    small[0].wait()
    small[1].wait()
    mean = jnp.sum(squares_ref[...], axis=1, keepdims=True) / float(width)
    scale_ref[...] = jnp.broadcast_to(lax.rsqrt(mean + 1e-05), (row_count, 128))

    def work(piece):
        copy(0, piece).wait()
        copy(2, piece).start()
        copy(1, piece).wait()
        at = pl.ds(pl.multiple_of(piece * tall, tall), tall)
        scale = scale_ref[at, :]
        for l in range(channels // 128):
            lanes = slice(l * 128, l * 128 + 128)
            summed = residual[at, lanes].astype(F32) + mixed[at, lanes].astype(F32)
            normed[at, lanes] = (summed * scale * gain_ref[:, lanes]).astype(BF16)
        copy(3, piece).start()

    loop(work)

    def drain(piece):
        copy(2, piece).wait()
        copy(3, piece).wait()

    loop(drain)


def shards(
    count, peers,
    query_proj, key_proj, value_proj, short_filter, residues, decay, skip_gain, residual, norm_gain
):
    rows, channels = query_proj.shape
    order = decay.shape[0]
    tap_count = short_filter.shape[1]
    tiles = channels // 128
    sub = min(8, tiles)
    groups = tiles // sub
    depth = count // 4
    wire = BF16 if sub == 8 else F32
    packet = (order * sub, 128) if wire == BF16 else (order, sub, 128)
    others = max(1, peers - 1)
    packets = pltpu.VMEM((groups, *packet), wire)
    modal = pltpu.VMEM((groups, order, sub, 128), F32)
    by_row = pltpu.VMEM((rows, groups, sub, 128), F32)
    dma = pltpu.SemaphoreType.DMA
    hbm = pl.BlockSpec(memory_space=pltpu.HBM)
    whole = pl.BlockSpec(memory_space=pltpu.VMEM)
    out = jax.ShapeDtypeStruct((rows, channels), BF16)
    mixed, squares = pl.pallas_call(
        functools.partial(kernel, count, peers, wire),
        out_shape=(out, jax.ShapeDtypeStruct((rows, 128), F32)),
        in_specs=[hbm] * 8,
        out_specs=(hbm, whole),
        scratch_shapes=[
            pltpu.VMEM((3, rows, channels), BF16),
            pltpu.VMEM((3, tap_count, channels), F32),
            pltpu.VMEM((order, channels), F32),
            pltpu.VMEM((order, channels), F32),
            pltpu.VMEM((groups, sub, 128), F32),
            pltpu.VMEM((rows, channels), BF16),
            pltpu.VMEM((3, 16, channels), BF16),
            pltpu.VMEM((3, groups, rows + 8, sub, 128), F32),
            pltpu.VMEM((3, 16 * sub, 128), F32),
            pltpu.VMEM((groups, 3, tap_count, sub, 128), F32),
            pltpu.VMEM((3 * tiles * 8, 128), F32),
            pltpu.VMEM((2, order * tiles, 128), F32),
            pltpu.VMEM((groups, 4, order, sub, 128), F32),
            modal,
            pltpu.VMEM((groups, 8, order, sub, 128), F32),
            pltpu.VMEM((groups, 8, sub, 128), F32),
            by_row, by_row,
            pltpu.VMEM((groups, rows // 8, order, sub, 128), F32),
            pltpu.VMEM((rows * tiles, 128), F32),
            pltpu.VMEM((rows, channels), BF16),
            modal, modal, modal, modal,
            pltpu.VMEM((order, sub, 128), F32),
            pltpu.VMEM((groups, 3 * sub * 8, 128), BF16),
            pltpu.VMEM((groups, 3 * sub * 8, 128), BF16),
            packets, packets, packets, packets, packets,
            pltpu.VMEM((groups, depth - 1, *packet), wire),
            pltpu.VMEM((rows, 128), F32), pltpu.VMEM((others, rows, 128), F32),
            dma((3, groups)), dma((5,)), dma((3,)), dma((rows // 16,)),
            dma((groups, 2)), dma((groups, 2)), dma((groups,)), dma((groups,)),
            dma((groups,)), dma((groups,)), dma((groups, depth - 1)), dma((groups, depth - 1)),
            dma((others,)), dma((others,)),
        ],
        compiler_params=pltpu.CompilerParams(
            collective_id=0, has_side_effects=True, vmem_limit_bytes=60 * 1024 * 1024
        ),
    )(
        query_proj, key_proj, value_proj, short_filter, residues, decay,
        skip_gain.reshape(groups, sub, 128), residual,
    )
    pieces = rows // 16
    block = pltpu.VMEM((rows, channels), BF16)
    return pl.pallas_call(
        functools.partial(normalise, channels * peers),
        out_shape=(out, out),
        in_specs=[hbm] * 4,
        out_specs=(hbm, hbm),
        scratch_shapes=[
            block, block, block, pltpu.VMEM((rows, 128), F32), pltpu.VMEM((1, channels), F32),
            pltpu.VMEM((rows, 128), F32), dma((2,)), dma((pieces,)), dma((pieces,)), dma((pieces,)), dma((pieces,))
        ],
        compiler_params=pltpu.CompilerParams(vmem_limit_bytes=60 * 1024 * 1024),
    )(mixed, residual, squares, norm_gain.reshape(1, channels))


def solution(mesh):
    in_specs = (
        P("context", "tensor"),
        P("context", "tensor"),
        P("context", "tensor"),
        P(None, None, "tensor"),
        P(None, "tensor"),
        P(None, "tensor"),
        P("tensor"),
        P("context", "tensor"),
        P("tensor"),
    )
    out_specs = (P("context", "tensor"), P("context", "tensor"))
    return jax.shard_map(
        functools.partial(shards, mesh.shape["context"], mesh.shape["tensor"]),
        mesh=mesh, in_specs=in_specs, out_specs=out_specs, check_vma=False,
    )
```

```python
import functools

import jax
import jax.numpy as jnp
from jax import lax
from jax.experimental import pallas as pl
from jax.experimental.pallas import tpu as pltpu
from jax.sharding import PartitionSpec as P

MESH = pl.DeviceIdType.MESH
F32 = jnp.float32
BF16 = jnp.bfloat16


def kernel(
    count, peers, wire,
    q_hbm, k_hbm, v_hbm, filter_hbm, residue_hbm, decay_hbm, skip_hbm, residual_hbm,
    mixed_hbm, squares_ref,
    inputs, filter_ref, residue_ref, decay_ref, skip_ref, residual_ref, edge,
    rows_x, turn, taps, taps_raw, modes, pole, weight, table, direct, prod, gate, starts, mix, mixed,
    state, first_ref, prefix, plane, column,
    halo_out, halo_in, x_out, x_in, y_out, y_in, z_out, z_in, sq_out, sq_in,
    in_sem, par_sem, edge_sem, out_sem,
    halo_ss, halo_rs, x_ss, x_rs, y_ss, y_rs, z_ss, z_rs, sq_ss, sq_rs,
):
    row_count, channels = q_hbm.shape
    tap_count = filter_hbm.shape[1]
    order = decay_hbm.shape[0]
    tiles = channels // 128
    sub = min(8, tiles)
    groups = tiles // sub
    blocks = row_count // 8
    several = 5 if (blocks - 1) % 5 == 0 else 1
    pitch = tiles * 8
    span = sub * 8
    me = lax.axis_index("context")
    side = lax.axis_index("tensor")
    x = lax.rem(me, 2)
    y = lax.rem(me // 2, 2)
    z = me // 4
    depth = count // 4
    x_peer = me + 1 - 2 * x
    y_peer = me + 2 - 4 * y
    has_prev, has_next = me > 0, me < count - 1

    sources = (q_hbm, k_hbm, v_hbm)

    def edge_copy(i):
        return pltpu.make_async_copy(
            sources[i].at[row_count - 16 : row_count], edge.at[i], edge_sem.at[i]
        )

    def input_copy(i, group):
        lanes = pl.ds(pl.multiple_of(group * sub * 128, 128), sub * 128)
        return pltpu.make_async_copy(
            sources[i].at[:, lanes], inputs.at[i, :, lanes], in_sem.at[i, group]
        )

    params = (
        (decay_hbm, decay_ref), (residue_hbm, residue_ref), (filter_hbm, filter_ref),
        (skip_hbm, skip_ref), (residual_hbm, residual_ref),
    )

    def param_copy(i):
        return pltpu.make_async_copy(params[i][0], params[i][1], par_sem.at[i])

    for i in range(3):
        edge_copy(i).start()
    for i in range(3):
        param_copy(i).start()
    for group in range(groups):
        input_copy(1, group).start()
        input_copy(2, group).start()
    for group in range(groups):
        input_copy(0, group).start()
    for i in range(3, 5):
        param_copy(i).start()

    barrier = pltpu.get_barrier_semaphore()

    def greet(context, tensor):
        pl.semaphore_signal(barrier, inc=1, device_id=(context, tensor), device_id_type=MESH)

    greet(x_peer, side)
    greet(y_peer, side)
    for shift in range(1, peers):
        greet(me, lax.rem(side + shift, peers))
    pl.when(has_prev)(lambda: greet(me - 1, side))
    pl.when(has_next)(lambda: greet(me + 1, side))
    for shift in range(1, depth):
        greet(lax.rem(me + 4 * shift, count), side)
    met = peers + depth + has_prev.astype(jnp.int32) + has_next.astype(jnp.int32)

    def loop(low, high, step):
        def body(index, carry):
            step(index)
            return carry

        lax.fori_loop(low, high, body, 0)

    def remote(src, dst, send, recv, context, tensor=side):
        return pltpu.make_async_remote_copy(
            src_ref=src, dst_ref=dst, send_sem=send, recv_sem=recv,
            device_id=(context, tensor), device_id_type=MESH,
        )

    def halo_copy(group, part):
        at = pl.ds(span, 2 * span) if part == 0 else pl.ds(0, span)
        return remote(
            halo_out.at[group, at], halo_in.at[group, at],
            halo_ss.at[group, part], halo_rs.at[group, part], lax.rem(me + 1, count),
        )

    def x_copy(group):
        return remote(x_out.at[group], x_in.at[group], x_ss.at[group], x_rs.at[group], x_peer)

    def y_copy(group):
        return remote(y_out.at[group], y_in.at[group], y_ss.at[group], y_rs.at[group], y_peer)

    def z_copy(group, shift):
        return remote(
            z_out.at[group], z_in.at[group, shift - 1],
            z_ss.at[group, shift - 1], z_rs.at[group, shift - 1],
            lax.rem(me + 4 * shift, count),
        )

    def to_wire(value):
        return value.reshape(order * sub, 128).astype(BF16) if wire == BF16 else value

    def from_wire(value):
        return value.astype(F32).reshape(order, sub, 128) if wire == BF16 else value

    for i in range(3):
        param_copy(i).wait()

    def spread(l):
        lanes = pl.ds(pl.multiple_of(l * 128, 128), 128)
        for i in range(3):
            base = pl.multiple_of((i * tiles + l) * 8, 8)
            taps_raw[pl.ds(base, tap_count), :] = filter_ref[i, :, lanes]
        for part in range(order // 8):
            base = pl.multiple_of((part * tiles + l) * 8, 8)
            modes[0, pl.ds(base, 8), :] = decay_ref[part * 8 : part * 8 + 8, lanes]
            modes[1, pl.ds(base, 8), :] = residue_ref[part * 8 : part * 8 + 8, lanes]

    loop(0, tiles, spread)

    def prepare(group):
        for i in range(3):
            for j in range(tap_count):
                start = i * pitch + group * span + j
                taps[group, i, j] = taps_raw[pl.ds(start, sub, stride=8), :]
        for m in range(order):
            start = ((m // 8) * tiles + group * sub) * 8 + m % 8
            rate = modes[0, pl.ds(start, sub, stride=8), :]
            residue = modes[1, pl.ds(start, sub, stride=8), :]
            pole[group, 0, m] = jnp.exp(-rate)
            pole[group, 1, m] = jnp.exp(-rate * float(row_count))
            pole[group, 2, m] = jnp.exp(-rate * float(row_count - 8))
            pole[group, 3, m] = jnp.exp(-rate * 8.0)
            weight[group, m] = residue * jnp.sqrt(1.0 - jnp.exp(-2.0 * rate))

    loop(0, groups, prepare)
    for i in range(3):
        edge_copy(i).wait()

    def pack(group):
        for i in range(3):
            for l in range(sub):
                lanes = pl.ds(pl.multiple_of((group * sub + l) * 128, 128), 128)
                last = edge[i, :, lanes].astype(F32)
                mix[(i * sub + l) * 8 : (i * sub + l + 1) * 8, :] = last[8:16]
        halo_out[group] = mix[0 : 3 * span, :].astype(BF16)

    loop(0, groups, pack)
    pl.semaphore_wait(barrier, met)

    @pl.when(has_next)
    def _():
        halo_copy(0, 0).start()

    def convolve(i, group, block):
        f = [taps[group, i, j] for j in range(tap_count)]
        rows = [rows_x[i, group, block * 8 + 8 + r] for r in range(1 - tap_count, 8)]
        outs = []
        for r in range(8):
            acc = rows[r + tap_count - 1] * f[0]
            for j in range(1, tap_count):
                acc = acc + rows[r + tap_count - 1 - j] * f[j]
            outs.append(acc)
        return outs

    def convert(chosen, group):
        for i in chosen:
            input_copy(i, group).wait()

        def body(pair, carry):
            at = pl.ds(pl.multiple_of(pair * 16, 16), 16)
            for i in chosen:
                for l in range(sub):
                    tile = group * sub + l
                    lanes = pl.ds(pl.multiple_of(tile * 128, 128), 128)
                    value = inputs[i, at, lanes].astype(F32)
                    for half in range(2):
                        start = half * span + l * 8
                        turn[i, start : start + 8, :] = value[half * 8 : half * 8 + 8]
            for i in chosen:
                for r in range(16):
                    start = (r // 8) * span + r % 8
                    rows_x[i, group, pair * 16 + 8 + r] = turn[i, pl.ds(start, sub, stride=8), :]
            return carry

        lax.fori_loop(0, blocks // 2, body, 0)

    def place_halo(chosen, group):
        @pl.when(has_prev)
        def _():
            for i in chosen:
                turn[i, 0:span, :] = halo_in[group, i * span : (i + 1) * span, :].astype(F32)
            for i in chosen:
                for r in range(8):
                    rows_x[i, group, r] = turn[i, pl.ds(r, sub, stride=8), :]

        @pl.when(jnp.logical_not(has_prev))
        def _():
            for i in chosen:
                rows_x[i, group, 0:8] = jnp.zeros((8, sub, 128), F32)

    def scan_block(group, block, h):
        keys = convolve(1, group, block)
        values = convolve(2, group, block)
        a = pole[group, 0]
        for r in range(8):
            p = keys[r] * values[r]
            prod[block * 8 + r, group] = p
            h = a * h + p[None]
        return h

    zero_state = jnp.zeros((order, sub, 128), F32)

    def phase_a(group):
        @pl.when(jnp.logical_and(has_next, group + 1 < groups))
        def _():
            halo_copy(group + 1, 0).start()

        convert((1, 2), group)

        def body(step, h):
            for k in range(several):
                block = 1 + step * several + k
                starts[group, block] = h
                h = scan_block(group, block, h)
            return h

        h = lax.fori_loop(0, (blocks - 1) // several, body, zero_state)
        state[group] = h
        pl.when(has_prev)(lambda: halo_copy(group, 0).wait_recv())
        place_halo((1, 2), group)
        first = scan_block(group, 0, zero_state)
        first_ref[group] = first
        e = state[group] + pole[group, 2] * first
        state[group] = e
        x_out[group] = to_wire(e)
        x_copy(group).start()
        pl.when(has_next)(lambda: halo_copy(group, 1).start())

    def stage_y(group):
        x_copy(group).wait_recv()
        other = from_wire(x_in[group])
        own = state[group]
        b = pole[group, 1]
        both = jnp.where(x == 1, b * other + own, b * own + other)
        prefix[group] = other * x.astype(F32)
        plane[group] = both
        y_out[group] = to_wire(both)
        y_copy(group).start()

    def stage_z(group):
        y_copy(group).wait_recv()
        other = from_wire(y_in[group])
        own = plane[group]
        b = pole[group, 1]
        b2 = b * b
        all4 = jnp.where(y == 1, b2 * other + own, b2 * own + other)
        here = prefix[group]
        prefix[group] = jnp.where(y == 1, here + jnp.where(x == 1, b, 1.0) * other, here)
        z_out[group] = to_wire(all4)
        for shift in range(1, depth):
            pl.when(z + shift < depth)(lambda shift=shift: z_copy(group, shift).start())

    def stage_end(group):
        b = pole[group, 1]
        b2 = b * b
        b4 = b2 * b2
        column[...] = zero_state
        for shift in range(depth - 1, 0, -1):

            @pl.when(z >= shift)
            def _(shift=shift):
                z_copy(group, shift).wait_recv()
                column[...] = b4 * column[...] + from_wire(z_in[group, shift - 1])

        scale = jnp.where(x == 1, b, 1.0) * jnp.where(y == 1, b2, 1.0)
        prefix[group] = prefix[group] + scale * column[...]

    def phase_b(group):
        convert((0,), group)
        pl.when(has_prev)(lambda: halo_copy(group, 1).wait_recv())
        place_halo((0,), group)

        def body(pair, carry):
            for k in range(2):
                block = pair * 2 + k
                gates = convolve(0, group, block)
                for r in range(8):
                    gate[block * 8 + r, group] = gates[r]
            return carry

        lax.fori_loop(0, blocks // 2, body, 0)
        a = pole[group, 0]
        w = weight[group]
        direct[group, 0] = jnp.sum(w, axis=0) + skip_ref[group]
        for r in range(8):
            w = w * a
            table[group, r] = w
            if r < 7:
                direct[group, r + 1] = jnp.sum(w, axis=0)

    def phase_c(group):
        def emit(block, s):
            p = [prod[block * 8 + r, group] for r in range(8)]
            for r in range(8):
                value = jnp.sum(table[group, r] * s, axis=0)
                near = direct[group, 0] * p[r]
                for j in range(1, r + 1):
                    near = near + direct[group, j] * p[r - j]
                start = block * pitch + group * span + r
                mix[pl.ds(start, sub, stride=8), :] = gate[block * 8 + r, group] * (value + near)

        a8 = pole[group, 3]
        s = prefix[group]
        emit(0, s)

        def body(step, s):
            for k in range(several):
                block = 1 + step * several + k
                emit(block, s + starts[group, block])
                s = pole[group, 3] * s
            return s

        lax.fori_loop(0, (blocks - 1) // several, body, a8 * s + first_ref[group])

    def forward(group):
        phase_a(group)
        pl.when(group >= 1)(lambda: stage_y(group - 1))
        pl.when(group >= 2)(lambda: stage_z(group - 2))

    def backward(group):
        stage_end(group)
        phase_c(group)

    loop(0, groups, forward)
    param_copy(3).wait()
    loop(0, groups // 2, phase_b)
    stage_y(groups - 1)
    if groups >= 2:
        stage_z(groups - 2)
    loop(groups // 2, groups, phase_b)
    stage_z(groups - 1)
    loop(0, groups, backward)
    param_copy(4).wait()

    def out_copy(pair):
        at = pl.ds(pl.multiple_of(pair * 16, 16), 16)
        return pltpu.make_async_copy(mixed.at[at], mixed_hbm.at[at], out_sem.at[pair])

    def finish(pair, carry):
        at = pl.ds(pl.multiple_of(pair * 16, 16), 16)
        squares = jnp.zeros((16, 128), F32)
        for l in range(tiles):
            parts = []
            for half in range(2):
                start = pl.multiple_of((pair * 2 + half) * pitch + l * 8, 8)
                parts.append(mix[pl.ds(start, 8), :])
            rounded = jnp.concatenate(parts, axis=0).astype(BF16)
            lanes = slice(l * 128, l * 128 + 128)
            mixed[at, lanes] = rounded
            summed = residual_ref[at, lanes].astype(F32) + rounded.astype(F32)
            squares = squares + summed * summed
        sq_out[at, :] = squares
        out_copy(pair).start()
        return carry

    lax.fori_loop(0, blocks // 2, finish, 0)

    def sq_copy(shift):
        return remote(
            sq_out, sq_in.at[shift - 1], sq_ss.at[shift - 1], sq_rs.at[shift - 1],
            me, lax.rem(side + shift, peers),
        )

    for shift in range(1, peers):
        sq_copy(shift).start()
    for shift in range(1, peers):
        sq_copy(shift).wait_recv()

    squares = sq_out[...]
    for shift in range(1, peers):
        squares = squares + sq_in[shift - 1]
    squares_ref[...] = squares

    def drain(pair, carry):
        out_copy(pair).wait()
        return carry

    lax.fori_loop(0, blocks // 2, drain, 0)
    for shift in range(1, peers):
        sq_copy(shift).wait_send()

    def settle(group):
        x_copy(group).wait_send()
        y_copy(group).wait_send()
        for shift in range(1, depth):
            pl.when(z + shift < depth)(lambda shift=shift: z_copy(group, shift).wait_send())

        @pl.when(has_next)
        def _():
            halo_copy(group, 0).wait_send()
            halo_copy(group, 1).wait_send()

    loop(0, groups, settle)


def normalise(
    width, mixed_hbm, residual_hbm, squares_hbm, gain_hbm, out_hbm, normed_hbm,
    mixed, residual, normed, squares_ref, gain_ref, scale_ref, small_sem, mixed_sem, residual_sem, out_sem, normed_sem,
):
    row_count, channels = mixed_hbm.shape
    tall = 16
    pieces = row_count // tall

    ends = (
        (mixed_hbm, mixed, mixed_sem), (residual_hbm, residual, residual_sem),
        (mixed, out_hbm, out_sem), (normed, normed_hbm, normed_sem),
    )

    def copy(kind, piece):
        source, target, sems = ends[kind]
        at = pl.ds(pl.multiple_of(piece * tall, tall), tall)
        return pltpu.make_async_copy(source.at[at], target.at[at], sems.at[piece])

    def loop(step):
        def body(index, carry):
            step(index)
            return carry

        lax.fori_loop(0, pieces, body, 0)

    def fetch(piece):
        copy(0, piece).start()
        copy(1, piece).start()

    small = (
        pltpu.make_async_copy(squares_hbm, squares_ref, small_sem.at[0]),
        pltpu.make_async_copy(gain_hbm, gain_ref, small_sem.at[1]),
    )
    small[0].start()
    small[1].start()
    loop(fetch)
    small[0].wait()
    small[1].wait()
    mean = jnp.sum(squares_ref[...], axis=1, keepdims=True) / float(width)
    scale_ref[...] = jnp.broadcast_to(lax.rsqrt(mean + 1e-05), (row_count, 128))

    def work(piece):
        copy(0, piece).wait()
        copy(2, piece).start()
        copy(1, piece).wait()
        at = pl.ds(pl.multiple_of(piece * tall, tall), tall)
        scale = scale_ref[at, :]
        for l in range(channels // 128):
            lanes = slice(l * 128, l * 128 + 128)
            summed = residual[at, lanes].astype(F32) + mixed[at, lanes].astype(F32)
            normed[at, lanes] = (summed * scale * gain_ref[:, lanes]).astype(BF16)
        copy(3, piece).start()

    loop(work)

    def drain(piece):
        copy(2, piece).wait()
        copy(3, piece).wait()

    loop(drain)


def shards(
    count, peers,
    query_proj, key_proj, value_proj, short_filter, residues, decay, skip_gain, residual, norm_gain
):
    rows, channels = query_proj.shape
    order = decay.shape[0]
    tap_count = short_filter.shape[1]
    tiles = channels // 128
    sub = min(8, tiles)
    groups = tiles // sub
    depth = count // 4
    wire = BF16 if sub == 8 else F32
    packet = (order * sub, 128) if wire == BF16 else (order, sub, 128)
    others = max(1, peers - 1)
    packets = pltpu.VMEM((groups, *packet), wire)
    modal = pltpu.VMEM((groups, order, sub, 128), F32)
    by_row = pltpu.VMEM((rows, groups, sub, 128), F32)
    dma = pltpu.SemaphoreType.DMA
    hbm = pl.BlockSpec(memory_space=pltpu.HBM)
    whole = pl.BlockSpec(memory_space=pltpu.VMEM)
    out = jax.ShapeDtypeStruct((rows, channels), BF16)
    mixed, squares = pl.pallas_call(
        functools.partial(kernel, count, peers, wire),
        out_shape=(out, jax.ShapeDtypeStruct((rows, 128), F32)),
        in_specs=[hbm] * 8,
        out_specs=(hbm, whole),
        scratch_shapes=[
            pltpu.VMEM((3, rows, channels), BF16),
            pltpu.VMEM((3, tap_count, channels), F32),
            pltpu.VMEM((order, channels), F32),
            pltpu.VMEM((order, channels), F32),
            pltpu.VMEM((groups, sub, 128), F32),
            pltpu.VMEM((rows, channels), BF16),
            pltpu.VMEM((3, 16, channels), BF16),
            pltpu.VMEM((3, groups, rows + 8, sub, 128), F32),
            pltpu.VMEM((3, 16 * sub, 128), F32),
            pltpu.VMEM((groups, 3, tap_count, sub, 128), F32),
            pltpu.VMEM((3 * tiles * 8, 128), F32),
            pltpu.VMEM((2, order * tiles, 128), F32),
            pltpu.VMEM((groups, 4, order, sub, 128), F32),
            modal,
            pltpu.VMEM((groups, 8, order, sub, 128), F32),
            pltpu.VMEM((groups, 8, sub, 128), F32),
            by_row, by_row,
            pltpu.VMEM((groups, rows // 8, order, sub, 128), F32),
            pltpu.VMEM((rows * tiles, 128), F32),
            pltpu.VMEM((rows, channels), BF16),
            modal, modal, modal, modal,
            pltpu.VMEM((order, sub, 128), F32),
            pltpu.VMEM((groups, 3 * sub * 8, 128), BF16),
            pltpu.VMEM((groups, 3 * sub * 8, 128), BF16),
            packets, packets, packets, packets, packets,
            pltpu.VMEM((groups, depth - 1, *packet), wire),
            pltpu.VMEM((rows, 128), F32), pltpu.VMEM((others, rows, 128), F32),
            dma((3, groups)), dma((5,)), dma((3,)), dma((rows // 16,)),
            dma((groups, 2)), dma((groups, 2)), dma((groups,)), dma((groups,)),
            dma((groups,)), dma((groups,)), dma((groups, depth - 1)), dma((groups, depth - 1)),
            dma((others,)), dma((others,)),
        ],
        compiler_params=pltpu.CompilerParams(
            collective_id=0, has_side_effects=True, vmem_limit_bytes=60 * 1024 * 1024
        ),
    )(
        query_proj, key_proj, value_proj, short_filter, residues, decay,
        skip_gain.reshape(groups, sub, 128), residual,
    )
    pieces = rows // 16
    block = pltpu.VMEM((rows, channels), BF16)
    return pl.pallas_call(
        functools.partial(normalise, channels * peers),
        out_shape=(out, out),
        in_specs=[hbm] * 4,
        out_specs=(hbm, hbm),
        scratch_shapes=[
            block, block, block, pltpu.VMEM((rows, 128), F32), pltpu.VMEM((1, channels), F32),
            pltpu.VMEM((rows, 128), F32), dma((2,)), dma((pieces,)), dma((pieces,)), dma((pieces,)), dma((pieces,))
        ],
        compiler_params=pltpu.CompilerParams(vmem_limit_bytes=60 * 1024 * 1024),
    )(mixed, residual, squares, norm_gain.reshape(1, channels))


def solution(mesh):
    in_specs = (
        P("context", "tensor"),
        P("context", "tensor"),
        P("context", "tensor"),
        P(None, None, "tensor"),
        P(None, "tensor"),
        P(None, "tensor"),
        P("tensor"),
        P("context", "tensor"),
        P("tensor"),
    )
    out_specs = (P("context", "tensor"), P("context", "tensor"))
    return jax.shard_map(
        functools.partial(shards, mesh.shape["context"], mesh.shape["tensor"]),
        mesh=mesh, in_specs=in_specs, out_specs=out_specs, check_vma=False,
    )
```
